512 devices in a mesh: row: 32 (over z, x), col: 16 (over y, core).
Axes of the slice: x: 4, y: 8, z: 8, core: 2. Of those that a mesh axis runs over, the one named last changes fastest.
Arguments:
- hidden: bfloat16 [4096, 12288], P('row', 'col'), may hold values from -6 to 6
- w_down: bfloat16 [12288, 4096], P('row', 'col'), may hold values from -0.0546875 to 0.0546875
- stream_in: bfloat16 [4096, 4096], P('row', 'col'), may hold values from -6 to 6
- w_qkv: bfloat16 [4096, 12288], P('row', 'col'), may hold values from -0.09375 to 0.09375
Outputs:
- stream: bfloat16 [4096, 4096], P('row', 'col')
- attended: bfloat16 [4096, 4096], P('row', 'col')
The draws below stay inside these ranges and needn't reach their ends.
All inputs are finite; a program needn't handle non-finite values.
Results may differ from the reference program's by a relative error of at most 0.015.
Values may be sent and summed in bfloat16 or wider, within the bound.
A program may use at most 64 MiB of HBM per device.

```python
import jax
import jax.numpy as jnp
from jax import lax

D_W = 4096
FF_W = 12288
HEAD = 128
PATCHES = 256
HEADS = 32
TOKENS = 4096
IMAGES = 16


def levels(key, shape, split, least, largest):
    gain = 1.0
    for dim, shards_of in split:
        steps = jax.random.uniform(jax.random.fold_in(jax.random.fold_in(key, 6), dim), (shards_of,), jnp.float32, least / len(split), largest / len(split))
        gain = gain * jnp.repeat(jnp.exp(steps), shape[dim] // shards_of).reshape((-1,) + (1,) * (len(shape) - 1 - dim))
    return gain


def noise(stream_key, shape, width, limit, split=(), dtype=jnp.bfloat16):
    level = levels(stream_key, shape, split, -0.22, 0.18) if split else 1.0
    values = jax.random.normal(stream_key, shape, jnp.float32) * width * level
    return jnp.minimum(jnp.maximum(values, -limit), limit).astype(dtype)


def setup_inputs(seed: int = 0) -> dict:
    seeds = jax.random.split(jax.random.key(seed), 5)
    return {
        "hidden": noise(seeds[0], (TOKENS, FF_W), 1.0, 6.0, ((0, 32), (1, 16))),
        "w_down": noise(seeds[1], (FF_W, D_W), FF_W ** -0.5, 0.0546875, ((0, 32), (1, 16))),
        "stream_in": noise(seeds[2], (TOKENS, D_W), 1.0, 6.0, ((0, 32), (1, 16))),
        "w_qkv": noise(seeds[3], (D_W, 3 * D_W), D_W ** -0.5, 0.09375, ((0, 32), (1, 16))),
    }


EPSILON = 1e-06

def head_norm(parts):
    centre = parts - lax.optimization_barrier(jnp.mean(parts, axis=-1, keepdims=True))
    spread = lax.optimization_barrier(jnp.mean(centre * centre, axis=-1, keepdims=True))
    return centre * jax.lax.rsqrt(spread + EPSILON)

def reference(hidden, w_down, stream_in, w_qkv):
    mlp_out = jnp.dot(hidden, w_down, preferred_element_type=jnp.float32)
    stream = (stream_in.astype(jnp.float32) + mlp_out).astype(jnp.bfloat16)
    stream_f32 = stream.astype(jnp.float32)
    row_mean = lax.optimization_barrier(jnp.sum(stream_f32, axis=1)) / D_W
    row_var = lax.optimization_barrier(jnp.sum(stream_f32 * stream_f32, axis=1)) / D_W - row_mean * row_mean
    normed = ((stream_f32 - row_mean[:, None]) * jax.lax.rsqrt(row_var + EPSILON)[:, None]).astype(jnp.bfloat16)
    qkv = jnp.dot(normed, w_qkv, preferred_element_type=jnp.float32).reshape(TOKENS, HEADS, 3, HEAD)
    queries = (head_norm(qkv[:, :, 0]) * (1.0 / HEAD ** 0.5)).astype(jnp.bfloat16)
    keys = head_norm(qkv[:, :, 1]).astype(jnp.bfloat16)
    values = qkv[:, :, 2].astype(jnp.bfloat16)
    queries = queries.reshape(IMAGES, PATCHES, HEADS, HEAD).astype(jnp.float32)
    keys = keys.reshape(IMAGES, PATCHES, HEADS, HEAD).astype(jnp.float32)
    values = values.reshape(IMAGES, PATCHES, HEADS, HEAD).astype(jnp.float32)
    scores = jnp.einsum('iqhe,ikhe->ihqk', queries, keys)
    expon = jnp.exp(scores)
    probs = (expon / lax.optimization_barrier(jnp.sum(expon, axis=-1, keepdims=True))).astype(jnp.bfloat16)
    attended = jnp.einsum('ihqk,ikhe->iqhe', probs.astype(jnp.float32), values)
    return (stream, attended.reshape(TOKENS, D_W).astype(jnp.bfloat16))
```

```python
import functools

import jax
import jax.numpy as jnp
from jax import lax
from jax.experimental import pallas as pl
from jax.experimental.pallas import tpu as pltpu
from jax.sharding import PartitionSpec as P

MESH = pl.DeviceIdType.MESH
EPSILON = 1e-06
D_W = 4096
HEAD = 128
NX, NY, NZ = 4, 8, 8
F32 = jnp.float32
BF16 = jnp.bfloat16


def head_norm(parts):
    centre = parts - jnp.mean(parts, axis=-1, keepdims=True)
    spread = jnp.mean(centre * centre, axis=-1, keepdims=True)
    return centre * lax.rsqrt(spread + EPSILON)


def kernel(
    hid, wd, si, wq, so, at,
    wdg, ag, p1, r1, sin, sg, st, stx, sty, wqg, p2, r2, ab,
    s_hid, r_hid, s_si, r_si, s_a, r_a, s_ac, r_ac, s_wd, r_wd, s_wq, r_wq, l_wd, l_wq,
    s_r1, r_r1, s_so, r_so, s_s, r_s, s_sc, r_sc, s_stx, r_stx, s_sty, r_sty, s_r2, r_r2, s_o, r_o,
):
    row, col = lax.axis_index("row"), lax.axis_index("col")
    z, x = lax.div(row, NX), lax.rem(row, NX)
    y, c = lax.div(col, 2), lax.rem(col, 2)
    xh, xl = lax.div(x, 2), lax.rem(x, 2)

    def dev(zz, xx, yy, cc):
        return (zz * NX + xx, yy * 2 + cc)

    up = lambda v, d, n: lax.rem(v + d + n, n)
    sibling = dev(z, x, y, 1 - c)
    yn = (dev(z, x, up(y, 1, NY), c), dev(z, x, up(y, -1, NY), c))
    zn = (dev(up(z, 1, NZ), x, y, c), dev(up(z, -1, NZ), x, y, c))
    xgroup = [dev(z, up(x, d, NX), y, e) for d in range(NX) for e in (c, 1 - c)][1:]
    ygroup = [dev(z, x, up(y, d, NY), c) for d in range(1, NY)]

    ends = []

    def remote(src, dst, ssem, rsem, to):
        copy = pltpu.make_async_remote_copy(
            src_ref=src, dst_ref=dst, send_sem=ssem, recv_sem=rsem, device_id=to, device_id_type=MESH
        )
        copy.start()
        ends.append((None, copy))

    def within(src, dst, ssem, rsem, tx, tc):
        away = (tx != x) | (tc != c)
        copy = pltpu.make_async_remote_copy(
            src_ref=src, dst_ref=dst, send_sem=ssem, recv_sem=rsem,
            device_id=dev(z, tx, y, tc), device_id_type=MESH,
        )

        @pl.when(away)
        def _():
            copy.start()

        @pl.when(jnp.logical_not(away))
        def _():
            pltpu.make_async_copy(src, dst, rsem).start()

        ends.append((away, copy))

    def arrived(dst, rsem):
        pltpu.make_async_remote_copy(
            src_ref=dst, dst_ref=dst, send_sem=rsem, recv_sem=rsem, device_id=sibling, device_id_type=MESH
        ).wait_recv()

    tok = lambda xt: pl.ds(pl.multiple_of(xt * 128, 128), 128)

    barrier = pltpu.get_barrier_semaphore()
    greet = xgroup + ygroup + list(zn)
    for d in greet:
        pl.semaphore_signal(barrier, inc=1, device_id=d, device_id_type=MESH)
    own_wd = pltpu.make_async_copy(wd, wdg.at[pl.ds(pl.multiple_of(z * 384, 128), 384)], l_wd.at[0])
    own_wd.start()
    own_wq = [
        pltpu.make_async_copy(
            wq.at[:, pl.ds(h * 384, 384)], wqg.at[h, pl.ds(pl.multiple_of(z * 128, 128), 128)], l_wq.at[h]
        )
        for h in range(2)
    ]
    for copy in own_wq:
        copy.start()
    pl.semaphore_wait(barrier, len(greet))

    def wd_piece(j, p):
        return wdg.at[pl.ds(pl.multiple_of(j * 384 + p * 192, 64), 192)]

    def wq_piece(j, p):
        return wqg.at[p, pl.ds(pl.multiple_of(j * 128, 128), 128)]

    def a_piece(j, i):
        return ag.at[j, tok(2 * i + c)]

    def s_piece(j, i):
        return sg.at[j, tok(2 * i + c)]

    def hop_send(piece, me, n, ssem, rsem, to, s, d, p, first=None):
        sign = 1 if d == 0 else -1
        j = up(me, -sign * (s - 1), n)
        k = (s - 1) * 4 + d * 2 + p
        remote(first(p) if s == 1 and first else piece(j, p), piece(j, p), ssem.at[k], rsem.at[k], to[d])

    def hop_wait(piece, me, n, rsem, s, d, p):
        sign = 1 if d == 0 else -1
        j = up(me, -sign * s, n)
        arrived(piece(j, p), rsem.at[(s - 1) * 4 + d * 2 + p])
        return j

    hops = lambda s: [(d, p) for p in range(2) for d in range(2) if s < 4 or d == p]

    for d, p in hops(1):
        hop_send(wd_piece, z, NZ, s_wd, r_wd, zn, 1, d, p, first=lambda p: wd.at[pl.ds(p * 192, 192)])
    for h in range(2):
        within(hid.at[:, pl.ds(h * 384, 384)], ag.at[y, tok(x)], s_hid.at[h], r_hid.at[xh], 2 * c + h, xl)
    for h in range(2):
        within(si.at[:, pl.ds(h * 128, 128)], sin.at[xh], s_si.at[h], r_si.at[xh], 2 * c + h, xl)
    for i in range(2):
        arrived(a_piece(y, i), r_hid.at[i])
        for d in range(2):
            hop_send(a_piece, y, NY, s_a, r_a, yn, 1, d, i)
        remote(a_piece(y, i), a_piece(y, i), s_ac.at[i], r_ac.at[i], sibling)

    def a_hop(s):
        for d, p in hops(s):
            j = hop_wait(a_piece, y, NY, r_a, s, d, p)
            if s < 4 and (s + 1 < 4 or d == p):
                hop_send(a_piece, y, NY, s_a, r_a, yn, s + 1, d, p)
            k = 2 + (s - 1) * 4 + d * 2 + p
            remote(a_piece(j, p), a_piece(j, p), s_ac.at[k], r_ac.at[k], sibling)

    def z_hop(piece, ssem, rsem, s):
        for d, p in hops(s):
            hop_wait(piece, z, NZ, rsem, s, d, p)
            if s < 4 and (s + 1 < 4 or d == p):
                hop_send(piece, z, NZ, ssem, rsem, zn, s + 1, d, p)

    for s in range(1, 5):
        z_hop(wd_piece, s_wd, r_wd, s)
        if s == 3:
            for copy in own_wq:
                copy.wait()
            for d, p in hops(1):
                hop_send(wq_piece, z, NZ, s_wq, r_wq, zn, 1, d, p)
        a_hop(s)
    own_wd.wait()

    def other_piece(j, i):
        return ag.at[j, tok(2 * i + 1 - c)]

    for i in range(2):
        arrived(other_piece(y, i), r_ac.at[i])
    for s in range(1, 5):
        for d, p in hops(s):
            j = up(y, -s if d == 0 else s, NY)
            arrived(other_piece(j, p), r_ac.at[2 + (s - 1) * 4 + d * 2 + p])

    for i in range(2):
        a = jnp.concatenate([ag[j, pl.ds(256 * i, 256), :] for j in range(NY)], axis=1)
        p1[pl.ds(256 * i, 256), :] = jnp.dot(a, wdg[...], preferred_element_type=F32).astype(BF16)
        for h in range(2):
            for e in range(2):
                within(
                    p1.at[tok(2 * i + e), pl.ds(128 * h, 128)], r1.at[x, i],
                    s_r1.at[i * 4 + h * 2 + e], r_r1.at[x * 2 + i], 2 * c + h, e,
                )

    z_hop(wq_piece, s_wq, r_wq, 1)

    lanes = lax.broadcasted_iota(jnp.int32, (8, 128), 0)
    ones = jnp.ones((8, 128), BF16)
    by_rows = lambda v: lax.dot_general(ones, v, (((1,), (1,)), ((), ())), preferred_element_type=F32)
    tile = jnp.zeros((8, 128), F32)
    for i in range(2):
        arrived(sin.at[i], r_si.at[i])
        total = sin[i].astype(F32)
        for xs in range(NX):
            arrived(r1.at[xs, i], r_r1.at[xs * 2 + i])
            total += r1[xs, i].astype(F32)
        block = total.astype(BF16)
        sg[y, tok(2 * i + c), :] = block
        for d in range(2):
            hop_send(s_piece, y, NY, s_s, r_s, yn, 1, d, i)
        remote(s_piece(y, i), s_piece(y, i), s_sc.at[i], r_sc.at[i], sibling)
        wide = block.astype(F32)
        square = wide * wide
        high = square.astype(BF16)
        low = (square - high.astype(F32)).astype(BF16)
        sums, squares = by_rows(block), by_rows(high) + by_rows(low)
        tile = jnp.where(lanes == i, sums, jnp.where(lanes == 2 + i, squares, tile))
    stx[c * 4 + x] = tile
    for n, d in enumerate(xgroup):
        remote(stx.at[c * 4 + x], stx.at[c * 4 + x], s_stx.at[n], r_stx.at[c * 4 + x], d)
    for i in range(2):
        within(s_piece(y, i), so.at[:, pl.ds(pl.multiple_of(128 * xl, 128), 128)], s_so.at[i], r_so.at[xl], 2 * i + c, xh)

    def s_hop(s):
        for d, p in hops(s):
            j = hop_wait(s_piece, y, NY, r_s, s, d, p)
            if s < 4 and (s + 1 < 4 or d == p):
                hop_send(s_piece, y, NY, s_s, r_s, yn, s + 1, d, p)
            k = 2 + (s - 1) * 4 + d * 2 + p
            remote(s_piece(j, p), s_piece(j, p), s_sc.at[k], r_sc.at[k], sibling)

    s_hop(1)
    for n in range(1, 2 * NX):
        k = lax.rem(c * 4 + x + n, 8)
        arrived(stx.at[k], r_stx.at[k])
    half = lambda k: (stx[4 * k] + stx[4 * k + 1]) + (stx[4 * k + 2] + stx[4 * k + 3])
    sty[y] = jnp.where(lanes < 4, half(0), jnp.concatenate([half(1)[4:8], half(1)[0:4]], axis=0))
    for n, d in enumerate(ygroup):
        remote(sty.at[y], sty.at[y], s_sty.at[n], r_sty.at[y], d)
    z_hop(wq_piece, s_wq, r_wq, 2)
    s_hop(2)
    s_hop(3)
    z_hop(wq_piece, s_wq, r_wq, 3)
    s_hop(4)
    for n in range(1, NY):
        k = lax.rem(y + n, NY)
        arrived(sty.at[k], r_sty.at[k])
    stats = sty[0]
    for j in range(1, NY):
        stats += sty[j]
    rows = []
    for xt in range(NX):
        i, k = xt // 2, xt % 2
        mean = stats[4 * k + i : 4 * k + i + 1] / D_W
        var = stats[4 * k + 2 + i : 4 * k + 3 + i] / D_W - mean * mean
        rows += [mean, lax.rsqrt(var + EPSILON)]
    st[...] = jnp.concatenate(rows + [jnp.zeros((120, 128), F32)], axis=0).T

    def other_s(j, i):
        return sg.at[j, tok(2 * i + 1 - c)]

    for i in range(2):
        arrived(other_s(y, i), r_sc.at[i])
    for s in range(1, 5):
        for d, p in hops(s):
            j = up(y, -s if d == 0 else s, NY)
            arrived(other_s(j, p), r_sc.at[2 + (s - 1) * 4 + d * 2 + p])
    z_hop(wq_piece, s_wq, r_wq, 4)

    for i in range(2):
        halves = []
        for k in range(2):
            xt = 2 * i + k
            mean, rstd = st[:, 2 * xt : 2 * xt + 1], st[:, 2 * xt + 1 : 2 * xt + 2]
            halves.append(
                jnp.concatenate(
                    [((sg[j, tok(xt), :].astype(F32) - mean) * rstd).astype(BF16) for j in range(NY)], axis=1
                )
            )
        normed = jnp.concatenate(halves, axis=0)
        for h in range(2):
            p2[h, i] = jnp.dot(normed, wqg[h], preferred_element_type=F32).astype(BF16)
            within(p2.at[h, i], r2.at[x], s_r2.at[2 * i + h], r_r2.at[x], 2 * c + h, i)

    total = jnp.zeros((256, 384), F32)
    for xs in range(NX):
        arrived(r2.at[xs], r_r2.at[xs])
        total += r2[xs].astype(F32)
    queries = (head_norm(total[:, 0:128]) * (1.0 / HEAD**0.5)).astype(BF16)
    keys = head_norm(total[:, 128:256]).astype(BF16)
    values = total[:, 256:384].astype(BF16)
    scores = lax.dot_general(queries, keys, (((1,), (1,)), ((), ())), preferred_element_type=F32)
    expon = jnp.exp(scores)
    probs = (expon / jnp.sum(expon, axis=-1, keepdims=True)).astype(BF16)
    ab[...] = jnp.dot(probs, values, preferred_element_type=F32).astype(BF16)
    for t in range(2):
        within(
            ab.at[pl.ds(128 * t, 128)], at.at[:, pl.ds(pl.multiple_of(128 * xl, 128), 128)],
            s_o.at[t], r_o.at[xl], 2 * c + t, xh,
        )

    for h in range(2):
        arrived(so.at[:, pl.ds(128 * h, 128)], r_so.at[h])
        arrived(at.at[:, pl.ds(128 * h, 128)], r_o.at[h])
    for away, copy in ends:
        if away is None:
            copy.wait_send()
        else:

            @pl.when(away)
            def _(copy=copy):
                copy.wait_send()


def shards(hidden, w_down, stream_in, w_qkv):
    dma = lambda *n: pltpu.SemaphoreType.DMA(n)
    vm = lambda *n: pltpu.VMEM(n, BF16)
    fm = lambda *n: pltpu.VMEM(n, F32)
    return pl.pallas_call(
        kernel,
        out_shape=(jax.ShapeDtypeStruct((128, 256), BF16), jax.ShapeDtypeStruct((128, 256), BF16)),
        in_specs=[pl.BlockSpec(memory_space=pltpu.VMEM)] * 4,
        out_specs=(pl.BlockSpec(memory_space=pltpu.VMEM),) * 2,
        scratch_shapes=[
            vm(3072, 256), vm(NY, 512, 384), vm(512, 256), vm(NX, 2, 128, 128), vm(2, 128, 128), vm(NY, 512, 128),
            fm(128, 128), fm(8, 8, 128), fm(NY, 8, 128), vm(2, 1024, 384), vm(2, 2, 256, 384), vm(NX, 256, 384),
            vm(256, 128),
            dma(2), dma(2), dma(2), dma(2), dma(16), dma(16), dma(18), dma(18), dma(16), dma(16), dma(16), dma(16),
            dma(1), dma(2),
            dma(8), dma(8), dma(2), dma(2), dma(16), dma(16), dma(18), dma(18), dma(7), dma(8), dma(7), dma(8),
            dma(4), dma(4), dma(2), dma(2),
        ],
        compiler_params=pltpu.CompilerParams(
            collective_id=0, has_side_effects=True, vmem_limit_bytes=40 * 1024 * 1024
        ),
        cost_estimate=pl.CostEstimate(flops=1_700_000_000, bytes_accessed=1_000_000, transcendentals=65536),
        name="layer",
    )(hidden, w_down, stream_in, w_qkv)


def solution(mesh):
    placed = (P("row", "col"),) * 4
    return jax.shard_map(
        shards, mesh=mesh, in_specs=placed, out_specs=(P("row", "col"), P("row", "col")), check_vma=False
    )
```

```python
import functools

import jax
import jax.numpy as jnp
from jax import lax
from jax.experimental import pallas as pl
from jax.experimental.pallas import tpu as pltpu
from jax.sharding import PartitionSpec as P

MESH = pl.DeviceIdType.MESH
EPSILON = 1e-06
D_W = 4096
HEAD = 128
NX, NY, NZ = 4, 8, 8
F32 = jnp.float32
BF16 = jnp.bfloat16


def head_norm(parts):
    centre = parts - jnp.mean(parts, axis=-1, keepdims=True)
    spread = jnp.mean(centre * centre, axis=-1, keepdims=True)
    return centre * lax.rsqrt(spread + EPSILON)


def kernel(
    hid, wd, si, wq, out,
    wdg, ag, p1, r1, sin, sg, st, stx, sty, wqg, p2, r2, ab, acc,

    s_hid, r_hid, s_si, r_si, s_a, r_a, s_ac, r_ac, s_wd, r_wd, s_wq, r_wq, l_wd, l_wq,
    s_r1, r_r1, s_so, r_so, s_s, r_s, s_sc, r_sc, s_stx, r_stx, s_sty, r_sty, s_r2, r_r2, s_o, r_o,
):
    so, at = out.at[0], out.at[1]
    row, col = lax.axis_index("row"), lax.axis_index("col")
    z, x = lax.div(row, NX), lax.rem(row, NX)
    y, c = lax.div(col, 2), lax.rem(col, 2)
    xh, xl = lax.div(x, 2), lax.rem(x, 2)

    def dev(zz, xx, yy, cc):
        return (zz * NX + xx, yy * 2 + cc)

    up = lambda v, d, n: lax.rem(v + d + n, n)
    sibling = dev(z, x, y, 1 - c)
    yn = (dev(z, x, up(y, 1, NY), c), dev(z, x, up(y, -1, NY), c))
    zn = (dev(up(z, 1, NZ), x, y, c), dev(up(z, -1, NZ), x, y, c))
    xgroup = [dev(z, up(x, d, NX), y, e) for d in range(NX) for e in (c, 1 - c)][1:]
    ygroup = [dev(z, x, up(y, d, NY), c) for d in range(1, NY)]

    ends = []

    def remote(src, dst, ssem, rsem, to):
        copy = pltpu.make_async_remote_copy(
            src_ref=src, dst_ref=dst, send_sem=ssem, recv_sem=rsem, device_id=to, device_id_type=MESH
        )
        copy.start()
        ends.append((None, copy))
        return copy

    def sent(copy):
        ends.remove((None, copy))
        copy.wait_send()

    def within(src, dst, ssem, rsem, tx, tc):
        away = (tx != x) | (tc != c)
        copy = pltpu.make_async_remote_copy(
            src_ref=src, dst_ref=dst, send_sem=ssem, recv_sem=rsem,
            device_id=dev(z, tx, y, tc), device_id_type=MESH,
        )

        @pl.when(away)
        def _():
            copy.start()

        @pl.when(jnp.logical_not(away))
        def _():
            pltpu.make_async_copy(src, dst, rsem).start()

        ends.append((away, copy))

    def arrived(dst, rsem):
        pltpu.make_async_remote_copy(
            src_ref=dst, dst_ref=dst, send_sem=rsem, recv_sem=rsem, device_id=sibling, device_id_type=MESH
        ).wait_recv()

    tok = lambda xt: pl.ds(pl.multiple_of(xt * 128, 128), 128)

    barrier = pltpu.get_barrier_semaphore()
    greet = xgroup + ygroup + list(zn)
    for d in greet:
        pl.semaphore_signal(barrier, inc=1, device_id=d, device_id_type=MESH)
    own = [pltpu.make_async_copy(wd, wdg.at[pl.ds(pl.multiple_of(z * 384, 128), 384)], l_wd.at[0])]
    for h in range(2):
        own.append(
            pltpu.make_async_copy(
                wq.at[:, pl.ds(h * 384, 384)], wqg.at[h, pl.ds(pl.multiple_of(z * 128, 128), 128)], l_wq.at[h]
            )
        )
    for copy in own:
        copy.start()
    own[0].wait()
    pl.semaphore_wait(barrier, len(greet))

    image = (xh, 1 - xh)

    def wd_piece(j, p):
        return wdg.at[pl.ds(pl.multiple_of(j * 384 + p * 192, 64), 192)]

    def wq_piece(j, p):
        return wqg.at[p, pl.ds(pl.multiple_of(j * 128, 128), 128)]

    def a_block(j, p, k=c):
        return ag.at[j, tok(2 * image[p] + k)]

    def a_piece(j, p):
        start = pl.multiple_of((2 * image[p // 2] + c) * 128 + p % 2 * 64, 64)
        return ag.at[j, pl.ds(start, 64)]

    def s_piece(j, p, k=c):
        return sg.at[j, tok(2 * image[p] + k)]

    def block(me, s, d, n):
        return up(me, -s if d == 0 else s, n)

    def hop_send(piece, me, n, ssem, rsem, to, s, d, p, parts=2):
        j, k = block(me, s - 1, d, n), ((s - 1) * 2 + d) * parts + p
        return remote(piece(j, p), piece(j, p), ssem.at[k], rsem.at[k], to[d])

    def hop(piece, me, n, ssem, rsem, to, s, p, parts=2):
        way = p * 2 // parts
        for d in (0, 1) if s < 4 else (way,):
            arrived(piece(block(me, s, d, n), p), rsem.at[((s - 1) * 2 + d) * parts + p])
            if s < 3 or (s == 3 and d == way):
                hop_send(piece, me, n, ssem, rsem, to, s + 1, d, p, parts)

    def share(piece, ssem, rsem, s, p):
        for d in ((0, 1) if 0 < s < 4 else (p,)):
            j, k = block(y, s, d, NY), s * 4 + d * 2 + p
            remote(piece(j, p), piece(j, p), ssem.at[k], rsem.at[k], sibling)

    def shared(piece, rsem, s, p):
        for d in ((0, 1) if 0 < s < 4 else (p,)):
            arrived(piece(block(y, s, d, NY), p, 1 - c), rsem.at[s * 4 + d * 2 + p])

    def wd_hop(s, p):
        hop(wd_piece, z, NZ, s_wd, r_wd, zn, s, p)

    def wq_hop(s):
        for p in range(2):
            hop(wq_piece, z, NZ, s_wq, r_wq, zn, s, p)

    def a_hop(s, p):
        for q in range(2):
            hop(a_piece, y, NY, s_a, r_a, yn, s, 2 * p + q, 4)
        share(a_block, s_ac, r_ac, s, p)

    for h in range(2):
        for q in range(2):
            within(
                hid.at[pl.ds(64 * q, 64), pl.ds(h * 384, 384)],
                ag.at[y, pl.ds(pl.multiple_of(x * 128 + 64 * q, 64), 64)],
                s_hid.at[2 * h + q], r_hid.at[2 * xh + q], 2 * c + h, xl,
            )
    first = [hop_send(wd_piece, z, NZ, s_wd, r_wd, zn, 1, d, 0) for d in range(2)]

    def a_start(p):
        for q in range(2):
            arrived(a_piece(y, 2 * p + q), r_hid.at[2 * image[p] + q])
            for d in range(2):
                hop_send(a_piece, y, NY, s_a, r_a, yn, 1, d, 2 * p + q, 4)
        share(a_block, s_ac, r_ac, 0, p)

    a_start(0)
    for d in range(2):
        sent(first[d])
        hop_send(wd_piece, z, NZ, s_wd, r_wd, zn, 1, d, 1)
    own[1].wait()
    own[2].wait()
    for s in range(1, 4):
        wd_hop(s, 0)
        if s == 3:
            hop_send(wq_piece, z, NZ, s_wq, r_wq, zn, 1, 1, 0)
        if s == 1:
            a_start(1)
            for h in range(2):
                within(
                    si.at[:, pl.ds(h * 128, 128)], sin.at[xh], s_si.at[h], r_si.at[xh], 2 * c + h, xl
                )
        else:
            a_hop(s - 1, 1)
        wd_hop(s, 1)
        if s == 3:
            hop_send(wq_piece, z, NZ, s_wq, r_wq, zn, 1, 0, 0)
        a_hop(s, 0)
    a_hop(3, 1)
    for s in range(4):
        for p in range(2):
            shared(a_block, r_ac, s, p)

    last_a = up(y, 4, NY)
    last_w = up(z, 4, NZ)
    last_w = jnp.where(last_w == last_a, up(last_a, 1, NY), last_w)
    gap = up(last_w - last_a, NY, NY)

    def early(k):
        return up(last_a, k + (gap <= k).astype(jnp.int32), NY)

    def product(i, js):
        a = jnp.concatenate([ag[j, pl.ds(256 * i, 256), :] for j in js], axis=1)
        w = jnp.concatenate([wdg[pl.ds(pl.multiple_of(j * 384, 128), 384), :] for j in js], axis=0)
        return jnp.dot(a, w, preferred_element_type=F32)

    for i in range(2):
        acc[pl.ds(256 * i, 256), :] = product(i, [early(k) for k in range(1, 7)])
    for p in range(2):
        wd_hop(4, p)
    for d in range(2):
        hop_send(wq_piece, z, NZ, s_wq, r_wq, zn, 1, d, 1)
    for p in range(2):
        a_hop(4, p)
    for p in range(2):
        shared(a_block, r_ac, 4, p)

    for i in range(2):
        rows = pl.ds(256 * i, 256)
        p1[rows, :] = (acc[rows, :] + product(i, [last_a, last_w])).astype(BF16)
        for h in range(2):
            for e in range(2):
                within(
                    p1.at[tok(2 * i + e), pl.ds(128 * h, 128)], r1.at[x, i],
                    s_r1.at[i * 4 + h * 2 + e], r_r1.at[x * 2 + i], 2 * c + h, e,
                )
    wq_hop(1)

    lanes = lax.broadcasted_iota(jnp.int32, (8, 128), 0)
    ones = jnp.ones((8, 128), BF16)
    by_rows = lambda v: lax.dot_general(ones, v, (((1,), (1,)), ((), ())), preferred_element_type=F32)
    tile = jnp.zeros((8, 128), F32)
    image = (0, 1)
    for i in range(2):
        arrived(sin.at[i], r_si.at[i])
        total = sin[i].astype(F32)
        for xs in range(NX):
            arrived(r1.at[xs, i], r_r1.at[xs * 2 + i])
            total += r1[xs, i].astype(F32)
        stream = total.astype(BF16)
        sg[y, tok(2 * i + c), :] = stream
        for d in range(2):
            hop_send(s_piece, y, NY, s_s, r_s, yn, 1, d, i)
        share(s_piece, s_sc, r_sc, 0, i)
        wide = stream.astype(F32)
        square = wide * wide
        high = square.astype(BF16)
        low = (square - high.astype(F32)).astype(BF16)
        sums, squares = by_rows(stream), by_rows(high) + by_rows(low)
        tile = jnp.where(lanes == i, sums, jnp.where(lanes == 2 + i, squares, tile))
    stx[c * 4 + x] = tile
    for n, d in enumerate(xgroup):
        remote(stx.at[c * 4 + x], stx.at[c * 4 + x], s_stx.at[n], r_stx.at[c * 4 + x], d)
    wq_hop(2)

    def s_hop(s, p):
        hop(s_piece, y, NY, s_s, r_s, yn, s, p)
        share(s_piece, s_sc, r_sc, s, p)

    s_hop(1, 0)
    s_hop(1, 1)
    for n in range(1, 2 * NX):
        k = lax.rem(c * 4 + x + n, 8)
        arrived(stx.at[k], r_stx.at[k])
    half = lambda k: (stx[4 * k] + stx[4 * k + 1]) + (stx[4 * k + 2] + stx[4 * k + 3])
    sty[y] = jnp.where(lanes < 4, half(0), jnp.concatenate([half(1)[4:8], half(1)[0:4]], axis=0))
    for n, d in enumerate(ygroup):
        remote(sty.at[y], sty.at[y], s_sty.at[n], r_sty.at[y], d)
    s_hop(2, 0)
    s_hop(2, 1)
    for i in range(2):
        within(s_piece(y, i), so.at[:, pl.ds(pl.multiple_of(128 * xl, 128), 128)], s_so.at[i], r_so.at[xl], 2 * i + c, xh)
    wq_hop(3)
    s_hop(3, 0)
    s_hop(3, 1)
    for n in range(1, NY):
        k = lax.rem(y + n, NY)
        arrived(sty.at[k], r_sty.at[k])
    stats = sty[0]
    for j in range(1, NY):
        stats += sty[j]
    rows = []
    for xt in range(NX):
        i, k = xt // 2, xt % 2
        mean = stats[4 * k + i : 4 * k + i + 1] / D_W
        var = stats[4 * k + 2 + i : 4 * k + 3 + i] / D_W - mean * mean
        rows += [mean, lax.rsqrt(var + EPSILON)]
    st[...] = jnp.concatenate(rows + [jnp.zeros((120, 128), F32)], axis=0).T
    wq_hop(4)

    for i in range(2):
        for s in range(4):
            shared(s_piece, r_sc, s, i)
        s_hop(4, i)
        shared(s_piece, r_sc, 4, i)
        halves = []
        for k in range(2):
            xt = 2 * i + k
            mean, rstd = st[:, 2 * xt : 2 * xt + 1], st[:, 2 * xt + 1 : 2 * xt + 2]
            halves.append(
                jnp.concatenate(
                    [((sg[j, tok(xt), :].astype(F32) - mean) * rstd).astype(BF16) for j in range(NY)], axis=1
                )
            )
        normed = jnp.concatenate(halves, axis=0)
        for h in range(2):
            p2[h, i] = jnp.dot(normed, wqg[h], preferred_element_type=F32).astype(BF16)
            within(p2.at[h, i], r2.at[x], s_r2.at[2 * i + h], r_r2.at[x], 2 * c + h, i)

    total = jnp.zeros((256, 384), F32)
    for xs in range(NX):
        arrived(r2.at[xs], r_r2.at[xs])
        total += r2[xs].astype(F32)
    queries = (head_norm(total[:, 0:128]) * (1.0 / HEAD**0.5)).astype(BF16)
    keys = head_norm(total[:, 128:256]).astype(BF16)
    values = total[:, 256:384].astype(BF16)
    scores = lax.dot_general(queries, keys, (((1,), (1,)), ((), ())), preferred_element_type=F32)
    expon = jnp.exp(scores)
    probs = (expon / jnp.sum(expon, axis=-1, keepdims=True)).astype(BF16)
    ab[...] = jnp.dot(probs, values, preferred_element_type=F32).astype(BF16)
    for t in range(2):
        within(
            ab.at[pl.ds(128 * t, 128)], at.at[:, pl.ds(pl.multiple_of(128 * xl, 128), 128)],
            s_o.at[t], r_o.at[xl], 2 * c + t, xh,
        )

    for h in range(2):
        arrived(so.at[:, pl.ds(128 * h, 128)], r_so.at[h])
        arrived(at.at[:, pl.ds(128 * h, 128)], r_o.at[h])
    for away, copy in ends:
        if away is None:
            copy.wait_send()
        else:

            @pl.when(away)
            def _(copy=copy):
                copy.wait_send()


def shards(hidden, w_down, stream_in, w_qkv):
    dma = lambda *n: pltpu.SemaphoreType.DMA(n)
    vm = lambda *n: pltpu.VMEM(n, BF16)
    fm = lambda *n: pltpu.VMEM(n, F32)
    out = pl.pallas_call(
        kernel,
        out_shape=jax.ShapeDtypeStruct((2, 128, 256), BF16),
        in_specs=[pl.BlockSpec(memory_space=pltpu.HBM)] * 4,
        out_specs=pl.BlockSpec(memory_space=pltpu.HBM),
        scratch_shapes=[
            vm(3072, 256), vm(NY, 512, 384), vm(512, 256), vm(NX, 2, 128, 128), vm(2, 128, 128), vm(NY, 512, 128),
            fm(128, 128), fm(8, 8, 128), fm(NY, 8, 128), vm(2, 1024, 384), vm(2, 2, 256, 384), vm(NX, 256, 384),
            vm(256, 128), fm(512, 256),
            dma(4), dma(4), dma(2), dma(2), dma(32), dma(32), dma(20), dma(20), dma(16), dma(16), dma(16), dma(16),
            dma(1), dma(2),
            dma(8), dma(8), dma(2), dma(2), dma(16), dma(16), dma(20), dma(20), dma(7), dma(8), dma(7), dma(8),
            dma(4), dma(4), dma(2), dma(2),
        ],
        compiler_params=pltpu.CompilerParams(
            collective_id=0, has_side_effects=True, vmem_limit_bytes=56 * 1024 * 1024
        ),
        cost_estimate=pl.CostEstimate(flops=1_700_000_000, bytes_accessed=1_000_000, transcendentals=65536),
        name="layer",
    )(hidden, w_down, stream_in, w_qkv)
    return out[0], out[1]


def solution(mesh):
    placed = (P("row", "col"),) * 4
    return jax.shard_map(
        shards, mesh=mesh, in_specs=placed, out_specs=(P("row", "col"), P("row", "col")), check_vma=False
    )
```

```python
import jax
import jax.numpy as jnp
from jax import lax
from jax.experimental import pallas as pl
from jax.experimental.pallas import tpu as pltpu
from jax.sharding import PartitionSpec as P

MESH = pl.DeviceIdType.MESH
EPSILON = 1e-06
D_W = 4096
HEAD = 128
NX, NY, NZ = 4, 8, 8
F32 = jnp.float32
BF16 = jnp.bfloat16


def head_norm(parts):
    centre = parts - jnp.mean(parts, axis=-1, keepdims=True)
    spread = jnp.mean(centre * centre, axis=-1, keepdims=True)
    return centre * lax.rsqrt(spread + EPSILON)


def kernel(
    hid, wd, si, wq, out,
    wdg, ag, acc, p1, r1, sin, sg, st, stx, sty, wqg, p2, r2, ab,
    s_hid, r_hid, s_si, r_si, s_a, r_a, s_wd, r_wd, s_wc, r_wc, s_wq, r_wq, s_qc, r_qc, own_sem,
    s_r1, r_r1, s_so, r_so, s_s, r_s, s_stx, r_stx, s_sty, r_sty, s_r2, r_r2, s_o, r_o,
):
    so, at = out.at[0], out.at[1]
    row, col = lax.axis_index("row"), lax.axis_index("col")
    z, x = lax.div(row, NX), lax.rem(row, NX)
    y, c = lax.div(col, 2), lax.rem(col, 2)
    xh, xl = lax.div(x, 2), lax.rem(x, 2)

    def dev(zz, xx, yy, cc):
        return (zz * NX + xx, yy * 2 + cc)

    def up(v, d, n):
        return lax.rem(v + d + n, n)

    sibling = dev(z, x, y, 1 - c)
    yn2 = (dev(z, x, up(y, 2, NY), c), dev(z, x, up(y, -2, NY), c))
    yn = (dev(z, x, up(y, 1, NY), c), dev(z, x, up(y, -1, NY), c))
    zn = (dev(up(z, 1, NZ), x, y, c), dev(up(z, -1, NZ), x, y, c))
    xgroup = [dev(z, up(x, d, NX), y, e) for d in range(NX) for e in (c, 1 - c)][1:]
    ygroup = [dev(z, x, up(y, d, NY), c) for d in range(1, NY)]
    away = (2, 1, 3)

    ends = []

    def remote(src, dst, ssem, rsem, to):
        copy = pltpu.make_async_remote_copy(
            src_ref=src, dst_ref=dst, send_sem=ssem, recv_sem=rsem, device_id=to, device_id_type=MESH
        )
        copy.start()
        ends.append((None, copy))

    def drain():
        for leaves, copy in ends:
            if leaves is None:
                copy.wait_send()
            else:

                @pl.when(leaves)
                def _(copy=copy):
                    copy.wait_send()

        ends.clear()

    def within(src, dst, ssem, rsem, tx, tc):
        leaves = (tx != x) | (tc != c)
        copy = pltpu.make_async_remote_copy(
            src_ref=src, dst_ref=dst, send_sem=ssem, recv_sem=rsem,
            device_id=dev(z, tx, y, tc), device_id_type=MESH,
        )

        @pl.when(leaves)
        def _():
            copy.start()

        @pl.when(jnp.logical_not(leaves))
        def _():
            pltpu.make_async_copy(src, dst, rsem).start()

        ends.append((leaves, copy))

    def arrived(dst, rsem):
        pltpu.make_async_remote_copy(
            src_ref=dst, dst_ref=dst, send_sem=rsem, recv_sem=rsem, device_id=sibling, device_id_type=MESH
        ).wait_recv()

    barrier = pltpu.get_barrier_semaphore()
    greet = xgroup + ygroup + list(zn)
    for d in greet:
        pl.semaphore_signal(barrier, inc=1, device_id=d, device_id_type=MESH)
    own = [pltpu.make_async_copy(wd, wdg.at[c, pl.ds(pl.multiple_of(z * 384, 128), 384)], own_sem.at[0])]
    for h in range(2):
        own.append(
            pltpu.make_async_copy(
                wq.at[:, pl.ds(h * 384, 384)],
                wqg.at[2 * c + h, pl.ds(pl.multiple_of(z * 128, 128), 128)],
                own_sem.at[1 + h],
            )
        )
    for copy in own:
        copy.start()
    own[0].wait()
    pl.semaphore_wait(barrier, len(greet))

    near = jnp.where(xh == c, xl, 1 - xl)
    half = (near, 1 - near)

    def wd_piece(j, p, k=c):
        return wdg.at[k, pl.ds(pl.multiple_of(j * 384 + p * 192, 64), 192)]

    def wq_piece(j, p, k=c):
        return wqg.at[2 * k + p, pl.ds(pl.multiple_of(j * 128, 128), 128)]

    def a_piece(j, p):
        return ag.at[j, pl.ds(pl.multiple_of(half[p // 2] * 128 + p % 2 * 64, 64), 64)]

    def s_piece(j, p):
        return sg.at[j, pl.ds(128 * p, 128)]

    def block(me, s, d):
        return up(me, -s if d == 0 else s, 8)

    def hop_send(piece, me, ssem, rsem, to, s, d, p, parts=2):
        j, k = block(me, s - 1, d), ((s - 1) * 2 + d) * parts + p
        remote(piece(j, p), piece(j, p), ssem.at[k], rsem.at[k], to[d])

    def hop(piece, me, ssem, rsem, to, s, p, parts=2):
        way = p * 2 // parts
        for d in (0, 1) if s < 4 else (way,):
            arrived(piece(block(me, s, d), p), rsem.at[((s - 1) * 2 + d) * parts + p])
            if s < 3 or (s == 3 and d == way):
                hop_send(piece, me, ssem, rsem, to, s + 1, d, p, parts)

    def share(piece, ssem, rsem, s, p):
        for d in (0, 1) if 0 < s < 4 else (p,):
            j, k = block(z, s, d), s * 4 + d * 2 + p
            remote(piece(j, p), piece(j, p), ssem.at[k], rsem.at[k], sibling)

    def shared(piece, rsem, s, p):
        for d in (0, 1) if 0 < s < 4 else (p,):
            arrived(piece(block(z, s, d), p, 1 - c), rsem.at[s * 4 + d * 2 + p])

    def wd_hop(s, p):
        hop(wd_piece, z, s_wd, r_wd, zn, s, p)
        share(wd_piece, s_wc, r_wc, s, p)

    def wq_start(d, p):
        hop_send(wq_piece, z, s_wq, r_wq, zn, 1, d, p)

    def wq_hop(s, ps=(0, 1)):
        for p in ps:
            hop(wq_piece, z, s_wq, r_wq, zn, s, p)
            share(wq_piece, s_qc, r_qc, s, p)

    def a_hop(s, p):
        for q in range(2):
            hop(a_piece, y, s_a, r_a, yn, s, 2 * p + q, 4)

    def a_start(p):
        for q in range(2):
            arrived(a_piece(y, 2 * p + q), r_hid.at[2 * half[p] + q])
            for d in range(2):
                hop_send(a_piece, y, s_a, r_a, yn, 1, d, 2 * p + q, 4)

    for h in range(2):
        for q in range(2):
            within(
                hid.at[pl.ds(64 * q, 64), pl.ds(h * 384, 384)],
                ag.at[y, pl.ds(pl.multiple_of(xl * 128 + 64 * q, 64), 64)],
                s_hid.at[2 * h + q], r_hid.at[2 * xl + q], 2 * c + h, xh,
            )
    for p in range(2):
        for d in range(2):
            hop_send(wd_piece, z, s_wd, r_wd, zn, 1, d, p)
    a_start(0)
    own[1].wait()
    own[2].wait()
    for p in range(2):
        share(wd_piece, s_wc, r_wc, 0, p)
    for s in range(1, 4):
        wd_hop(s, 0)
        if s == 1:
            a_start(1)
            for h in range(2):
                within(si.at[:, pl.ds(h * 128, 128)], sin.at[xl], s_si.at[h], r_si.at[xl], 2 * c + h, xh)
        else:
            a_hop(s - 1, 1)
        wd_hop(s, 1)
        if s > 1:
            for d in range(2):
                wq_start(d, s - 2)
        a_hop(s, 0)
    a_hop(3, 1)
    wq_hop(1, (0,))
    for s in range(4):
        for p in range(2):
            shared(wd_piece, r_wc, s, p)

    last_a, last_w = up(y, 4, 8), up(z, 4, 8)
    last_w = jnp.where(last_w == last_a, up(last_a, 1, 8), last_w)
    gap = up(last_w - last_a, 8, 8)

    def product(n, js):
        a = jnp.concatenate([ag[j] for j in js], axis=1)
        w = jnp.concatenate([wdg[n, pl.ds(pl.multiple_of(j * 384, 128), 384), :] for j in js], axis=0)
        return jnp.dot(a, w, preferred_element_type=F32)

    early = [up(last_a, k + (gap <= k).astype(jnp.int32), 8) for k in range(1, 7)]
    for n in range(2):
        acc[n] = product(n, early)
    for p in range(2):
        wd_hop(4, p)
    wq_hop(1, (1,))
    for p in range(2):
        shared(wd_piece, r_wc, 4, p)
    for p in range(2):
        a_hop(4, p)

    for n in range(2):
        p1[:, pl.ds(256 * n, 256)] = (acc[n] + product(n, [last_a, last_w])).astype(BF16)

    def features(tx):
        return pl.ds(pl.multiple_of(128 * tx, 128), 128)

    for k, d in enumerate(away):
        tx = up(x, d, NX)
        remote(p1.at[:, features(tx)], r1.at[k], s_r1.at[k], r_r1.at[k], dev(z, tx, y, c))
    for p in range(2):
        share(wq_piece, s_qc, r_qc, 0, p)
    wq_hop(2)

    lanes = lax.broadcasted_iota(jnp.int32, (8, 128), 0)
    ones = jnp.ones((8, 128), BF16)

    def by_rows(v):
        return lax.dot_general(ones, v, (((1,), (1,)), ((), ())), preferred_element_type=F32)

    for t in range(2):
        arrived(sin.at[t], r_si.at[t])
    for k in range(3):
        arrived(r1.at[k], r_r1.at[k])

    def s_send(j, s, d, p, to):
        k = (s - 1) * 4 + d * 2 + p
        remote(s_piece(j, p), s_piece(j, p), s_s.at[k], r_s.at[k], to[d])

    def s_hop(s):
        for p in range(2):
            for d in (0, 1) if s < 4 else (p,):
                j = block(y, s, d)
                arrived(s_piece(j, p), r_s.at[(s - 1) * 4 + d * 2 + p])
                if s == 2:
                    s_send(j, 3, d, p, yn)
                    if d == p:
                        s_send(j, 4, d, p, yn2)

    tile = jnp.zeros((8, 128), F32)
    for t in range(2):
        rows = pl.ds(128 * t, 128)
        total = sin[t].astype(F32) + p1[rows, features(x)].astype(F32)
        for k in range(3):
            total += r1[k, rows, :].astype(F32)
        stream = total.astype(BF16)
        sg[y, rows, :] = stream
        for d in range(2):
            s_send(y, 2, d, t, yn2)
        for d in range(2):
            s_send(y, 1, d, t, yn)
        wide = stream.astype(F32)
        square = wide * wide
        high = square.astype(BF16)
        low = (square - high.astype(F32)).astype(BF16)
        sums, squares = by_rows(stream), by_rows(high) + by_rows(low)
        tile = jnp.where(lanes == t, sums, jnp.where(lanes == 2 + t, squares, tile))
    stx[3] = tile
    for k, d in enumerate(away):
        remote(stx.at[3], stx.at[k], s_stx.at[k], r_stx.at[k], dev(z, up(x, d, NX), y, c))
    wq_hop(3)
    s_hop(2)
    for k in range(3):
        arrived(stx.at[k], r_stx.at[k])
    sty[y] = (stx[0] + stx[1]) + (stx[2] + stx[3])
    for n, d in enumerate(ygroup):
        remote(sty.at[y], sty.at[y], s_sty.at[n], r_sty.at[y], d)
    wq_hop(4)
    s_hop(1)
    for t in range(2):
        within(s_piece(y, t), so.at[:, pl.ds(pl.multiple_of(128 * xl, 128), 128)], s_so.at[t], r_so.at[xl], 2 * c + t, xh)
    s_hop(3)
    for n in range(1, NY):
        k = up(y, n, NY)
        arrived(sty.at[k], r_sty.at[k])
    stats = sty[0]
    for j in range(1, NY):
        stats += sty[j]
    means = stats[0:2] / D_W
    spreads = lax.rsqrt(stats[2:4] / D_W - means * means + EPSILON)
    st[...] = jnp.concatenate([means, spreads, jnp.zeros((124, 128), F32)], axis=0).T
    for s in range(5):
        for p in range(2):
            shared(wq_piece, r_qc, s, p)
    s_hop(4)

    halves = []
    for t in range(2):
        mean, rstd = st[:, t : t + 1], st[:, 2 + t : 3 + t]
        halves.append(
            jnp.concatenate(
                [((sg[j, pl.ds(128 * t, 128), :].astype(F32) - mean) * rstd).astype(BF16) for j in range(NY)],
                axis=1,
            )
        )
    normed = jnp.concatenate(halves, axis=0)
    for k, d in enumerate(away):
        tx = up(x, d, NX)
        p2[k] = jnp.dot(normed, wqg[tx], preferred_element_type=F32).astype(BF16)
        remote(p2.at[k], r2.at[k], s_r2.at[k], r_r2.at[k], dev(z, tx, y, c))
    total = jnp.dot(normed, wqg[x], preferred_element_type=F32)
    sent = ends[-3:]
    del ends[-3:]
    drain()
    ends.extend(sent)
    for k in range(3):
        arrived(r2.at[k], r_r2.at[k])
        total += r2[k].astype(F32)
    queries = (head_norm(total[:, 0:128]) * (1.0 / HEAD**0.5)).astype(BF16)
    keys = head_norm(total[:, 128:256]).astype(BF16)
    values = total[:, 256:384].astype(BF16)
    scores = lax.dot_general(queries, keys, (((1,), (1,)), ((), ())), preferred_element_type=F32)
    expon = jnp.exp(scores)
    probs = (expon / jnp.sum(expon, axis=-1, keepdims=True)).astype(BF16)
    ab[...] = jnp.dot(probs, values, preferred_element_type=F32).astype(BF16)
    for t in range(2):
        within(
            ab.at[pl.ds(128 * t, 128)], at.at[:, pl.ds(pl.multiple_of(128 * xl, 128), 128)],
            s_o.at[t], r_o.at[xl], 2 * c + t, xh,
        )

    for h in range(2):
        arrived(so.at[:, pl.ds(128 * h, 128)], r_so.at[h])
        arrived(at.at[:, pl.ds(128 * h, 128)], r_o.at[h])
    drain()


def shards(hidden, w_down, stream_in, w_qkv):
    vm = lambda *n: pltpu.VMEM(n, BF16)
    fm = lambda *n: pltpu.VMEM(n, F32)
    counts = (4, 4, 2, 2, 32, 32, 16, 16, 20, 20, 16, 16, 20, 20, 3, 3, 3, 2, 2, 16, 16, 3, 3, 7, 8, 3, 3, 2, 2)
    out = pl.pallas_call(
        kernel,
        out_shape=jax.ShapeDtypeStruct((2, 128, 256), BF16),
        in_specs=[pl.BlockSpec(memory_space=pltpu.HBM)] * 4,
        out_specs=pl.BlockSpec(memory_space=pltpu.HBM),
        scratch_shapes=[
            vm(2, 3072, 256), vm(8, 256, 384), fm(2, 256, 256), vm(256, 512), vm(3, 256, 128), vm(2, 128, 128),
            vm(8, 256, 128), fm(128, 128), fm(4, 8, 128), fm(8, 8, 128), vm(4, 1024, 384), vm(3, 256, 384),
            vm(3, 256, 384), vm(256, 128),
            *(pltpu.SemaphoreType.DMA((n,)) for n in counts),
        ],
        compiler_params=pltpu.CompilerParams(
            collective_id=0, has_side_effects=True, vmem_limit_bytes=56 * 1024 * 1024
        ),
        cost_estimate=pl.CostEstimate(flops=1_700_000_000, bytes_accessed=1_000_000, transcendentals=65536),
        name="layer",
    )(hidden, w_down, stream_in, w_qkv)
    return out[0], out[1]


def solution(mesh):
    placed = (P("row", "col"),) * 4
    return jax.shard_map(
        shards, mesh=mesh, in_specs=placed, out_specs=(P("row", "col"), P("row", "col")), check_vma=False
    )
```

```python
import jax
import jax.numpy as jnp
from jax import lax
from jax.experimental import pallas as pl
from jax.experimental.pallas import tpu as pltpu
from jax.sharding import PartitionSpec as P

MESH = pl.DeviceIdType.MESH
EPSILON = 1e-06
D_W = 4096
HEAD = 128
NX, NY, NZ = 4, 8, 8
F32 = jnp.float32
BF16 = jnp.bfloat16


def head_norm(parts):
    centre = parts - jnp.mean(parts, axis=-1, keepdims=True)
    spread = jnp.mean(centre * centre, axis=-1, keepdims=True)
    return centre * lax.rsqrt(spread + EPSILON)


def kernel(
    hid, wd, si, wq, out,
    wdg, ag, acc, p1, r1, sin, sg, st, stx, sty, wqg, p2, r2, ab, keep,
    s_hid, r_hid, s_si, r_si, s_a, r_a, s_wd, r_wd, s_wc, r_wc, s_wq, r_wq, s_qc, r_qc, own_sem,
    s_r1, r_r1, s_so, r_so, s_s, r_s, s_stx, r_stx, s_sty, r_sty, s_r2, r_r2, s_o, r_o,
):
    so, at = out.at[0], out.at[1]
    row, col = lax.axis_index("row"), lax.axis_index("col")
    z, x = lax.div(row, NX), lax.rem(row, NX)
    y, c = lax.div(col, 2), lax.rem(col, 2)
    xh, xl = lax.div(x, 2), lax.rem(x, 2)

    def dev(zz, xx, yy, cc):
        return (zz * NX + xx, yy * 2 + cc)

    def up(v, d, n):
        return lax.rem(v + d + n, n)

    sibling = dev(z, x, y, 1 - c)
    yn2 = (dev(z, x, up(y, 2, NY), c), dev(z, x, up(y, -2, NY), c))
    yn = (dev(z, x, up(y, 1, NY), c), dev(z, x, up(y, -1, NY), c))
    zn = (dev(up(z, 1, NZ), x, y, c), dev(up(z, -1, NZ), x, y, c))
    xgroup = [dev(z, up(x, d, NX), y, e) for d in range(NX) for e in (c, 1 - c)][1:]
    ygroup = [dev(z, x, up(y, d, NY), c) for d in range(1, NY)]
    away = (2, 1, 3)

    ends = []

    def remote(src, dst, ssem, rsem, to):
        copy = pltpu.make_async_remote_copy(
            src_ref=src, dst_ref=dst, send_sem=ssem, recv_sem=rsem, device_id=to, device_id_type=MESH
        )
        copy.start()
        ends.append((None, copy))

    def drain():
        for leaves, copy in ends:
            if leaves is None:
                copy.wait_send()
            else:

                @pl.when(leaves)
                def _(copy=copy):
                    copy.wait_send()

        ends.clear()

    def within(src, dst, ssem, rsem, tx, tc):
        leaves = (tx != x) | (tc != c)
        copy = pltpu.make_async_remote_copy(
            src_ref=src, dst_ref=dst, send_sem=ssem, recv_sem=rsem,
            device_id=dev(z, tx, y, tc), device_id_type=MESH,
        )

        @pl.when(leaves)
        def _():
            copy.start()

        @pl.when(jnp.logical_not(leaves))
        def _():
            pltpu.make_async_copy(src, dst, rsem).start()

        ends.append((leaves, copy))

    def arrived(dst, rsem):
        pltpu.make_async_remote_copy(
            src_ref=dst, dst_ref=dst, send_sem=rsem, recv_sem=rsem, device_id=sibling, device_id_type=MESH
        ).wait_recv()

    barrier = pltpu.get_barrier_semaphore()
    greet = xgroup + ygroup + list(zn)
    for d in greet:
        pl.semaphore_signal(barrier, inc=1, device_id=d, device_id_type=MESH)
    own = [pltpu.make_async_copy(wd, wdg.at[c, pl.ds(pl.multiple_of(z * 384, 128), 384)], own_sem.at[0])]
    for h in range(2):
        own.append(
            pltpu.make_async_copy(
                wq.at[:, pl.ds(h * 384, 384)],
                wqg.at[2 * c + h, pl.ds(pl.multiple_of(z * 128, 128), 128)],
                own_sem.at[1 + h],
            )
        )
    for copy in own:
        copy.start()
    own[0].wait()
    pl.semaphore_wait(barrier, len(greet))

    near = jnp.where(xh == c, xl, 1 - xl)
    half = (near, 1 - near)

    def wd_piece(j, p, k=c):
        return wdg.at[k, pl.ds(pl.multiple_of(j * 384 + p * 192, 64), 192)]

    def wq_piece(j, p, k=c):
        return wqg.at[2 * k + p, pl.ds(pl.multiple_of(j * 128, 128), 128)]

    def a_piece(j, p):
        return ag.at[j, pl.ds(pl.multiple_of(half[p // 2] * 128 + p % 2 * 64, 64), 64)]

    def s_piece(j, p):
        return sg.at[j, pl.ds(128 * p, 128)]

    def block(me, s, d):
        return up(me, -s if d == 0 else s, 8)

    def hop_send(piece, me, ssem, rsem, to, s, d, p, parts=2):
        j, k = block(me, s - 1, d), ((s - 1) * 2 + d) * parts + p
        remote(piece(j, p), piece(j, p), ssem.at[k], rsem.at[k], to[d])

    def hop(piece, me, ssem, rsem, to, s, p, parts=2):
        way = p * 2 // parts
        for d in (0, 1) if s < 4 else (way,):
            arrived(piece(block(me, s, d), p), rsem.at[((s - 1) * 2 + d) * parts + p])
            if s < 3 or (s == 3 and d == way):
                hop_send(piece, me, ssem, rsem, to, s + 1, d, p, parts)

    def share(piece, ssem, rsem, s, p):
        for d in (0, 1) if 0 < s < 4 else (p,):
            j, k = block(z, s, d), s * 4 + d * 2 + p
            remote(piece(j, p), piece(j, p), ssem.at[k], rsem.at[k], sibling)

    def shared(piece, rsem, s, p):
        for d in (0, 1) if 0 < s < 4 else (p,):
            arrived(piece(block(z, s, d), p, 1 - c), rsem.at[s * 4 + d * 2 + p])

    def wd_hop(s, p):
        hop(wd_piece, z, s_wd, r_wd, zn, s, p)
        share(wd_piece, s_wc, r_wc, s, p)

    def wq_start(d, p):
        hop_send(wq_piece, z, s_wq, r_wq, zn, 1, d, p)

    def wq_hop(s, ps=(0, 1)):
        for p in ps:
            hop(wq_piece, z, s_wq, r_wq, zn, s, p)
            share(wq_piece, s_qc, r_qc, s, p)

    def a_hop(s, p):
        for q in range(2):
            hop(a_piece, y, s_a, r_a, yn, s, 2 * p + q, 4)

    def a_start(p):
        for q in range(2):
            arrived(a_piece(y, 2 * p + q), r_hid.at[2 * half[p] + q])
            for d in range(2):
                hop_send(a_piece, y, s_a, r_a, yn, 1, d, 2 * p + q, 4)

    for h in range(2):
        for q in range(2):
            within(
                hid.at[pl.ds(64 * q, 64), pl.ds(h * 384, 384)],
                ag.at[y, pl.ds(pl.multiple_of(xl * 128 + 64 * q, 64), 64)],
                s_hid.at[2 * h + q], r_hid.at[2 * xl + q], 2 * c + h, xh,
            )
    for p in range(2):
        for d in range(2):
            hop_send(wd_piece, z, s_wd, r_wd, zn, 1, d, p)
    a_start(0)
    a_start(1)
    own[1].wait()
    own[2].wait()
    for p in range(2):
        share(wd_piece, s_wc, r_wc, 0, p)
    for h in range(2):
        within(si.at[:, pl.ds(h * 128, 128)], sin.at[xl], s_si.at[h], r_si.at[xl], 2 * c + h, xh)
    for s in range(1, 4):
        wd_hop(s, 0)
        if s > 1:
            a_hop(s - 1, 1)
        wd_hop(s, 1)
        if s > 1:
            for d in range(2):
                wq_start(d, s - 2)
        a_hop(s, 0)
    a_hop(3, 1)
    wq_hop(1, (0,))
    for s in range(4):
        for p in range(2):
            shared(wd_piece, r_wc, s, p)

    last_a, last_w = up(y, 4, 8), up(z, 4, 8)
    last_w = jnp.where(last_w == last_a, up(last_a, 1, 8), last_w)
    gap = up(last_w - last_a, 8, 8)

    def product(n, js, rows=slice(None)):
        a = jnp.concatenate([ag[j, rows] for j in js], axis=1)
        w = jnp.concatenate([wdg[n, pl.ds(pl.multiple_of(j * 384, 128), 384), :] for j in js], axis=0)
        return jnp.dot(a, w, preferred_element_type=F32)

    early = [up(last_a, k + (gap <= k).astype(jnp.int32), 8) for k in range(1, 7)]
    for n in range(2):
        acc[n] = product(n, early)
    for p in range(2):
        wd_hop(4, p)
    wq_hop(1, (1,))
    for p in range(2):
        shared(wd_piece, r_wc, 4, p)
    for p in range(2):
        a_hop(4, p)

    def features(tx):
        return pl.ds(pl.multiple_of(128 * tx, 128), 128)

    halves = (pl.ds(0, 128), pl.ds(128, 128))
    for t, rows in enumerate(halves):
        for n in range(2):
            late = product(n, [last_a, last_w], rows)
            p1[rows, pl.ds(256 * n, 256)] = (acc[n, rows] + late).astype(BF16)
        for k, d in enumerate(away):
            tx = up(x, d, NX)
            remote(
                p1.at[rows, features(tx)], r1.at[k, rows], s_r1.at[3 * t + k], r_r1.at[3 * t + k], dev(z, tx, y, c)
            )
    for p in range(2):
        share(wq_piece, s_qc, r_qc, 0, p)
    wq_hop(2)

    lanes = lax.broadcasted_iota(jnp.int32, (8, 128), 0)
    ones = jnp.ones((8, 128), BF16)

    def by_rows(v):
        return lax.dot_general(ones, v, (((1,), (1,)), ((), ())), preferred_element_type=F32)


    def s_send(j, s, d, p, to):
        k = (s - 1) * 4 + d * 2 + p
        remote(s_piece(j, p), s_piece(j, p), s_s.at[k], r_s.at[k], to[d])

    def s_hop(s, p):
        for d in (0, 1) if s < 4 else (p,):
            j = block(y, s, d)
            arrived(s_piece(j, p), r_s.at[(s - 1) * 4 + d * 2 + p])
            if s == 2:
                s_send(j, 3, d, p, yn)
                if d == p:
                    s_send(j, 4, d, p, yn2)

    tile = jnp.zeros((8, 128), F32)
    for t, rows in enumerate(halves):
        arrived(sin.at[t], r_si.at[t])
        for k in range(3):
            arrived(r1.at[k, rows], r_r1.at[3 * t + k])
        total = sin[t].astype(F32) + p1[rows, features(x)].astype(F32)
        for k in range(3):
            total += r1[k, rows, :].astype(F32)
        stream = total.astype(BF16)
        sg[y, rows, :] = stream
        for d in range(2):
            s_send(y, 2, d, t, yn2)
        for d in range(2):
            s_send(y, 1, d, t, yn)
        wide = stream.astype(F32)
        square = wide * wide
        high = square.astype(BF16)
        low = (square - high.astype(F32)).astype(BF16)
        sums, squares = by_rows(stream), by_rows(high) + by_rows(low)
        tile = jnp.where(lanes == t, sums, jnp.where(lanes == 2 + t, squares, tile))
    stx[3] = tile
    for k, d in enumerate(away):
        remote(stx.at[3], stx.at[k], s_stx.at[k], r_stx.at[k], dev(z, up(x, d, NX), y, c))
    wq_hop(3)
    s_hop(2, 0)
    for k in range(3):
        arrived(stx.at[k], r_stx.at[k])
    sty[y] = (stx[0] + stx[1]) + (stx[2] + stx[3])
    for n, d in enumerate(ygroup):
        remote(sty.at[y], sty.at[y], s_sty.at[n], r_sty.at[y], d)
    s_hop(2, 1)
    for t in range(2):
        within(s_piece(y, t), so.at[:, pl.ds(pl.multiple_of(128 * xl, 128), 128)], s_so.at[t], r_so.at[xl], 2 * c + t, xh)
    wq_hop(4)
    for s in (1, 3, 4):
        s_hop(s, 0)
    for n in range(1, NY):
        k = up(y, n, NY)
        arrived(sty.at[k], r_sty.at[k])
    stats = sty[0]
    for j in range(1, NY):
        stats += sty[j]
    means = stats[0:2] / D_W
    spreads = lax.rsqrt(stats[2:4] / D_W - means * means + EPSILON)
    st[...] = jnp.concatenate([means, spreads, jnp.zeros((124, 128), F32)], axis=0).T
    for s in range(5):
        for p in range(2):
            shared(wq_piece, r_qc, s, p)

    for t, rows in enumerate(halves):
        if t == 1:
            for s in (1, 3, 4):
                s_hop(s, 1)
        mean, rstd = st[:, t : t + 1], st[:, 2 + t : 3 + t]
        normed = jnp.concatenate(
            [((sg[j, rows, :].astype(F32) - mean) * rstd).astype(BF16) for j in range(NY)], axis=1
        )
        for k, d in enumerate(away):
            tx = up(x, d, NX)
            p2[k, rows, :] = jnp.dot(normed, wqg[tx], preferred_element_type=F32).astype(BF16)
            remote(p2.at[k, rows], r2.at[k, rows], s_r2.at[3 * t + k], r_r2.at[3 * t + k], dev(z, tx, y, c))
        keep[rows, :] = jnp.dot(normed, wqg[x], preferred_element_type=F32)
    sent = ends[-6:]
    del ends[-6:]
    drain()
    ends.extend(sent)
    for t, rows in enumerate(halves):
        for k in range(3):
            arrived(r2.at[k, rows], r_r2.at[3 * t + k])
        keep[rows, :] += (r2[0, rows].astype(F32) + r2[1, rows].astype(F32)) + r2[2, rows].astype(F32)
    total = keep[...]
    keys = head_norm(total[:, 128:256]).astype(BF16)
    values = total[:, 256:384].astype(BF16)
    for t in range(2):
        queries = (head_norm(total[128 * t : 128 * t + 128, 0:128]) * (1.0 / HEAD**0.5)).astype(BF16)
        scores = lax.dot_general(queries, keys, (((1,), (1,)), ((), ())), preferred_element_type=F32)
        expon = jnp.exp(scores)
        probs = (expon / jnp.sum(expon, axis=-1, keepdims=True)).astype(BF16)
        ab[pl.ds(128 * t, 128), :] = jnp.dot(probs, values, preferred_element_type=F32).astype(BF16)
        within(
            ab.at[pl.ds(128 * t, 128)], at.at[:, pl.ds(pl.multiple_of(128 * xl, 128), 128)],
            s_o.at[t], r_o.at[xl], 2 * c + t, xh,
        )

    for h in range(2):
        arrived(so.at[:, pl.ds(128 * h, 128)], r_so.at[h])
        arrived(at.at[:, pl.ds(128 * h, 128)], r_o.at[h])
    drain()


def shards(hidden, w_down, stream_in, w_qkv):
    vm = lambda *n: pltpu.VMEM(n, BF16)
    fm = lambda *n: pltpu.VMEM(n, F32)
    counts = (4, 4, 2, 2, 32, 32, 16, 16, 20, 20, 16, 16, 20, 20, 3, 6, 6, 2, 2, 16, 16, 3, 3, 7, 8, 6, 6, 2, 2)
    out = pl.pallas_call(
        kernel,
        out_shape=jax.ShapeDtypeStruct((2, 128, 256), BF16),
        in_specs=[pl.BlockSpec(memory_space=pltpu.HBM)] * 4,
        out_specs=pl.BlockSpec(memory_space=pltpu.HBM),
        scratch_shapes=[
            vm(2, 3072, 256), vm(8, 256, 384), fm(2, 256, 256), vm(256, 512), vm(3, 256, 128), vm(2, 128, 128),
            vm(8, 256, 128), fm(128, 128), fm(4, 8, 128), fm(8, 8, 128), vm(4, 1024, 384), vm(3, 256, 384),
            vm(3, 256, 384), vm(256, 128), fm(256, 384),
            *(pltpu.SemaphoreType.DMA((n,)) for n in counts),
        ],
        compiler_params=pltpu.CompilerParams(
            collective_id=0, has_side_effects=True, vmem_limit_bytes=56 * 1024 * 1024
        ),
        cost_estimate=pl.CostEstimate(flops=1_700_000_000, bytes_accessed=1_000_000, transcendentals=65536),
        name="layer",
    )(hidden, w_down, stream_in, w_qkv)
    return out[0], out[1]


def solution(mesh):
    placed = (P("row", "col"),) * 4
    return jax.shard_map(
        shards, mesh=mesh, in_specs=placed, out_specs=(P("row", "col"), P("row", "col")), check_vma=False
    )
```

```python
import jax
import jax.numpy as jnp
from jax import lax
from jax.experimental import pallas as pl
from jax.experimental.pallas import tpu as pltpu
from jax.sharding import PartitionSpec as P

MESH = pl.DeviceIdType.MESH
EPSILON = 1e-06
D_W = 4096
HEAD = 128
NX, NY, NZ = 4, 8, 8
F32 = jnp.float32
BF16 = jnp.bfloat16


def head_norm(parts):
    centre = parts - jnp.mean(parts, axis=-1, keepdims=True)
    spread = jnp.mean(centre * centre, axis=-1, keepdims=True)
    return centre * lax.rsqrt(spread + EPSILON)


def kernel(
    hid, wd, si, wq, out,
    wdg, ag, acc, p1, r1, sin, sg, st, stx, sty, wqg, p2, r2, ab, keep,
    s_hid, r_hid, s_si, r_si, s_a, r_a, s_wd, r_wd, s_wc, r_wc, s_wq, r_wq, s_qc, r_qc, own_sem,
    s_r1, r_r1, s_so, r_so, s_s, r_s, s_stx, r_stx, s_sty, r_sty, s_r2, r_r2, s_o, r_o,
):
    so, at = out.at[0], out.at[1]
    row, col = lax.axis_index("row"), lax.axis_index("col")
    z, x = lax.div(row, NX), lax.rem(row, NX)
    y, c = lax.div(col, 2), lax.rem(col, 2)
    xh, xl = lax.div(x, 2), lax.rem(x, 2)

    def dev(zz, xx, yy, cc):
        return (zz * NX + xx, yy * 2 + cc)

    def up(v, d, n):
        return lax.rem(v + d + n, n)

    sibling = dev(z, x, y, 1 - c)
    yn2 = (dev(z, x, up(y, 2, NY), c), dev(z, x, up(y, -2, NY), c))
    yn = (dev(z, x, up(y, 1, NY), c), dev(z, x, up(y, -1, NY), c))
    zn = (dev(up(z, 1, NZ), x, y, c), dev(up(z, -1, NZ), x, y, c))
    xgroup = [dev(z, up(x, d, NX), y, e) for d in range(NX) for e in (c, 1 - c)][1:]
    ygroup = [dev(z, x, up(y, d, NY), c) for d in range(1, NY)]
    away = (2, 1, 3)

    ends = []

    def remote(src, dst, ssem, rsem, to):
        copy = pltpu.make_async_remote_copy(
            src_ref=src, dst_ref=dst, send_sem=ssem, recv_sem=rsem, device_id=to, device_id_type=MESH
        )
        copy.start()
        ends.append((None, copy))

    def drain():
        for leaves, copy in ends:
            if leaves is None:
                copy.wait_send()
            else:

                @pl.when(leaves)
                def _(copy=copy):
                    copy.wait_send()

        ends.clear()

    def within(src, dst, ssem, rsem, tx, tc):
        leaves = (tx != x) | (tc != c)
        copy = pltpu.make_async_remote_copy(
            src_ref=src, dst_ref=dst, send_sem=ssem, recv_sem=rsem,
            device_id=dev(z, tx, y, tc), device_id_type=MESH,
        )

        @pl.when(leaves)
        def _():
            copy.start()

        @pl.when(jnp.logical_not(leaves))
        def _():
            pltpu.make_async_copy(src, dst, rsem).start()

        ends.append((leaves, copy))

    def arrived(dst, rsem):
        pltpu.make_async_remote_copy(
            src_ref=dst, dst_ref=dst, send_sem=rsem, recv_sem=rsem, device_id=sibling, device_id_type=MESH
        ).wait_recv()

    barrier = pltpu.get_barrier_semaphore()
    greet = xgroup + ygroup + list(zn)
    for d in greet:
        pl.semaphore_signal(barrier, inc=1, device_id=d, device_id_type=MESH)
    own = [pltpu.make_async_copy(wd, wdg.at[c, pl.ds(pl.multiple_of(z * 384, 128), 384)], own_sem.at[0])]
    for h in range(2):
        own.append(
            pltpu.make_async_copy(
                wq.at[:, pl.ds(h * 384, 384)],
                wqg.at[2 * c + h, pl.ds(pl.multiple_of(z * 128, 128), 128)],
                own_sem.at[1 + h],
            )
        )
    for copy in own:
        copy.start()
    own[0].wait()
    pl.semaphore_wait(barrier, len(greet))

    near = jnp.where(xh == c, xl, 1 - xl)
    half = (near, 1 - near)

    def wd_piece(j, p, k=c):
        return wdg.at[k, pl.ds(pl.multiple_of(j * 384 + p * 192, 64), 192)]

    def wq_piece(j, p, k=c):
        return wqg.at[2 * k + p, pl.ds(pl.multiple_of(j * 128, 128), 128)]

    def a_piece(j, p):
        return ag.at[j, pl.ds(pl.multiple_of(half[p // 2] * 128 + p % 2 * 64, 64), 64)]

    def s_piece(j, p):
        return sg.at[j, pl.ds(128 * p, 128)]

    def block(me, s, d):
        return up(me, -s if d == 0 else s, 8)

    def hop_send(piece, me, ssem, rsem, to, s, d, p, parts=2):
        j, k = block(me, s - 1, d), ((s - 1) * 2 + d) * parts + p
        remote(piece(j, p), piece(j, p), ssem.at[k], rsem.at[k], to[d])

    def hop(piece, me, ssem, rsem, to, s, p, parts=2):
        way = p * 2 // parts
        for d in (0, 1) if s < 4 else (way,):
            arrived(piece(block(me, s, d), p), rsem.at[((s - 1) * 2 + d) * parts + p])
            if s < 3 or (s == 3 and d == way):
                hop_send(piece, me, ssem, rsem, to, s + 1, d, p, parts)

    def share(piece, ssem, rsem, s, p):
        for d in (0, 1) if 0 < s < 4 else (p,):
            j, k = block(z, s, d), s * 4 + d * 2 + p
            remote(piece(j, p), piece(j, p), ssem.at[k], rsem.at[k], sibling)

    def shared(piece, rsem, s, p):
        for d in (0, 1) if 0 < s < 4 else (p,):
            arrived(piece(block(z, s, d), p, 1 - c), rsem.at[s * 4 + d * 2 + p])

    def wd_hop(s, p):
        hop(wd_piece, z, s_wd, r_wd, zn, s, p)
        share(wd_piece, s_wc, r_wc, s, p)

    def wq_start(d, p):
        hop_send(wq_piece, z, s_wq, r_wq, zn, 1, d, p)

    def wq_hop(s, ps=(0, 1)):
        for p in ps:
            hop(wq_piece, z, s_wq, r_wq, zn, s, p)
            share(wq_piece, s_qc, r_qc, s, p)

    def a_hop(s, p):
        for q in range(2):
            hop(a_piece, y, s_a, r_a, yn, s, 2 * p + q, 4)

    def a_start(p):
        for q in range(2):
            arrived(a_piece(y, 2 * p + q), r_hid.at[2 * half[p] + q])
            for d in range(2):
                hop_send(a_piece, y, s_a, r_a, yn, 1, d, 2 * p + q, 4)

    for h in range(2):
        for q in range(2):
            within(
                hid.at[pl.ds(64 * q, 64), pl.ds(h * 384, 384)],
                ag.at[y, pl.ds(pl.multiple_of(xl * 128 + 64 * q, 64), 64)],
                s_hid.at[2 * h + q], r_hid.at[2 * xl + q], 2 * c + h, xh,
            )
    for p in range(2):
        for d in range(2):
            hop_send(wd_piece, z, s_wd, r_wd, zn, 1, d, p)
    a_start(0)
    a_start(1)
    own[1].wait()
    own[2].wait()
    for p in range(2):
        share(wd_piece, s_wc, r_wc, 0, p)
    for h in range(2):
        within(si.at[:, pl.ds(h * 128, 128)], sin.at[xl], s_si.at[h], r_si.at[xl], 2 * c + h, xh)
    for s in range(1, 4):
        wd_hop(s, 0)
        if s > 1:
            a_hop(s - 1, 1)
        wd_hop(s, 1)
        if s > 1:
            for d in range(2):
                wq_start(d, s - 2)
        a_hop(s, 0)
    a_hop(3, 1)
    wq_hop(1, (0,))
    for s in range(4):
        for p in range(2):
            shared(wd_piece, r_wc, s, p)

    last_a, last_w = up(y, 4, 8), up(z, 4, 8)
    last_w = jnp.where(last_w == last_a, up(last_a, 1, 8), last_w)
    gap = up(last_w - last_a, 8, 8)

    def product(n, js, rows=slice(None)):
        a = jnp.concatenate([ag[j, rows] for j in js], axis=1)
        w = jnp.concatenate([wdg[n, pl.ds(pl.multiple_of(j * 384, 128), 384), :] for j in js], axis=0)
        return jnp.dot(a, w, preferred_element_type=F32)

    early = [up(last_a, k + (gap <= k).astype(jnp.int32), 8) for k in range(1, 7)]
    for n in range(2):
        acc[n] = product(n, early)
    for p in range(2):
        wd_hop(4, p)
    wq_hop(1, (1,))
    for p in range(2):
        shared(wd_piece, r_wc, 4, p)
    for p in range(2):
        a_hop(4, p)

    def features(tx):
        return pl.ds(pl.multiple_of(128 * tx, 128), 128)

    halves = (pl.ds(0, 128), pl.ds(128, 128))
    for t, rows in enumerate(halves):
        for n in range(2):
            late = product(n, [last_a, last_w], rows)
            p1[rows, pl.ds(256 * n, 256)] = (acc[n, rows] + late).astype(BF16)
        for k, d in enumerate(away):
            tx = up(x, d, NX)
            remote(
                p1.at[rows, features(tx)], r1.at[k, rows], s_r1.at[3 * t + k], r_r1.at[3 * t + k], dev(z, tx, y, c)
            )
    for p in range(2):
        share(wq_piece, s_qc, r_qc, 0, p)
    wq_hop(2)

    lanes = lax.broadcasted_iota(jnp.int32, (8, 128), 0)
    ones = jnp.ones((8, 128), BF16)

    def by_rows(v):
        return lax.dot_general(ones, v, (((1,), (1,)), ((), ())), preferred_element_type=F32)


    def s_send(j, s, d, p, to):
        k = (s - 1) * 4 + d * 2 + p
        remote(s_piece(j, p), s_piece(j, p), s_s.at[k], r_s.at[k], to[d])

    def s_hop(s, p):
        for d in (0, 1) if s < 4 else (p,):
            j = block(y, s, d)
            arrived(s_piece(j, p), r_s.at[(s - 1) * 4 + d * 2 + p])
            if s == 2:
                s_send(j, 3, d, p, yn)
                if d == p:
                    s_send(j, 4, d, p, yn2)

    tile = jnp.zeros((8, 128), F32)
    for t, rows in enumerate(halves):
        arrived(sin.at[t], r_si.at[t])
        for k in range(3):
            arrived(r1.at[k, rows], r_r1.at[3 * t + k])
        total = sin[t].astype(F32) + p1[rows, features(x)].astype(F32)
        for k in range(3):
            total += r1[k, rows, :].astype(F32)
        stream = total.astype(BF16)
        sg[y, rows, :] = stream
        for d in range(2):
            s_send(y, 2, d, t, yn2)
        for d in range(2):
            s_send(y, 1, d, t, yn)
        wide = stream.astype(F32)
        square = wide * wide
        high = square.astype(BF16)
        low = (square - high.astype(F32)).astype(BF16)
        sums, squares = by_rows(stream), by_rows(high) + by_rows(low)
        tile = jnp.where(lanes == t, sums, jnp.where(lanes == 2 + t, squares, tile))
    stx[3] = tile
    for k, d in enumerate(away):
        remote(stx.at[3], stx.at[k], s_stx.at[k], r_stx.at[k], dev(z, up(x, d, NX), y, c))
    wq_hop(3)
    s_hop(2, 0)
    for k in range(3):
        arrived(stx.at[k], r_stx.at[k])
    sty[y] = (stx[0] + stx[1]) + (stx[2] + stx[3])
    for n, d in enumerate(ygroup):
        remote(sty.at[y], sty.at[y], s_sty.at[n], r_sty.at[y], d)
    s_hop(2, 1)
    for t in range(2):
        within(s_piece(y, t), so.at[:, pl.ds(pl.multiple_of(128 * xl, 128), 128)], s_so.at[t], r_so.at[xl], 2 * c + t, xh)
    wq_hop(4)
    for s in (1, 3, 4):
        s_hop(s, 0)
    for n in range(1, NY):
        k = up(y, n, NY)
        arrived(sty.at[k], r_sty.at[k])
    stats = sty[0]
    for j in range(1, NY):
        stats += sty[j]
    means = stats[0:2] / D_W
    spreads = lax.rsqrt(stats[2:4] / D_W - means * means + EPSILON)
    st[...] = jnp.concatenate([means, spreads, jnp.zeros((124, 128), F32)], axis=0).T
    for s in range(5):
        for p in range(2):
            shared(wq_piece, r_qc, s, p)

    for t, rows in enumerate(halves):
        if t == 1:
            for s in (1, 3, 4):
                s_hop(s, 1)
        mean, rstd = st[:, t : t + 1], st[:, 2 + t : 3 + t]
        normed = jnp.concatenate(
            [((sg[j, rows, :].astype(F32) - mean) * rstd).astype(BF16) for j in range(NY)], axis=1
        )
        for k, d in enumerate(away):
            tx = up(x, d, NX)
            p2[k, rows, :] = jnp.dot(normed, wqg[tx], preferred_element_type=F32).astype(BF16)
            remote(p2.at[k, rows], r2.at[k, rows], s_r2.at[3 * t + k], r_r2.at[3 * t + k], dev(z, tx, y, c))
        keep[rows, :] = jnp.dot(normed, wqg[x], preferred_element_type=F32)
    sent = ends[-6:]
    del ends[-6:]
    drain()
    ends.extend(sent)
    for t, rows in enumerate(halves):
        for k in range(3):
            arrived(r2.at[k, rows], r_r2.at[3 * t + k])
        keep[rows, :] += (r2[0, rows].astype(F32) + r2[1, rows].astype(F32)) + r2[2, rows].astype(F32)
    total = keep[...]
    keys = head_norm(total[:, 128:256]).astype(BF16)
    values = total[:, 256:384].astype(BF16)
    for t in range(2):
        queries = (head_norm(total[128 * t : 128 * t + 128, 0:128]) * (1.0 / HEAD**0.5)).astype(BF16)
        scores = lax.dot_general(queries, keys, (((1,), (1,)), ((), ())), preferred_element_type=F32)
        expon = jnp.exp(scores)
        probs = (expon / jnp.sum(expon, axis=-1, keepdims=True)).astype(BF16)
        ab[pl.ds(128 * t, 128), :] = jnp.dot(probs, values, preferred_element_type=F32).astype(BF16)
        within(
            ab.at[pl.ds(128 * t, 128)], at.at[:, pl.ds(pl.multiple_of(128 * xl, 128), 128)],
            s_o.at[t], r_o.at[xl], 2 * c + t, xh,
        )

    for h in range(2):
        arrived(so.at[:, pl.ds(128 * h, 128)], r_so.at[h])
        arrived(at.at[:, pl.ds(128 * h, 128)], r_o.at[h])
    drain()


def shards(hidden, w_down, stream_in, w_qkv):
    vm = lambda *n: pltpu.VMEM(n, BF16)
    fm = lambda *n: pltpu.VMEM(n, F32)
    counts = (4, 4, 2, 2, 32, 32, 16, 16, 20, 20, 16, 16, 20, 20, 3, 6, 6, 2, 2, 16, 16, 3, 3, 7, 8, 6, 6, 2, 2)
    out = pl.pallas_call(
        kernel,
        out_shape=pltpu.VMEM((2, 128, 256), BF16),
        in_specs=[pl.BlockSpec(memory_space=pltpu.HBM)] * 4,
        out_specs=pl.BlockSpec(memory_space=pltpu.VMEM),
        scratch_shapes=[
            vm(2, 3072, 256), vm(8, 256, 384), fm(2, 256, 256), vm(256, 512), vm(3, 256, 128), vm(2, 128, 128),
            vm(8, 256, 128), fm(128, 128), fm(4, 8, 128), fm(8, 8, 128), vm(4, 1024, 384), vm(3, 256, 384),
            vm(3, 256, 384), vm(256, 128), fm(256, 384),
            *(pltpu.SemaphoreType.DMA((n,)) for n in counts),
        ],
        compiler_params=pltpu.CompilerParams(
            collective_id=0, has_side_effects=True, vmem_limit_bytes=56 * 1024 * 1024
        ),
        cost_estimate=pl.CostEstimate(flops=1_700_000_000, bytes_accessed=1_000_000, transcendentals=65536),
        name="layer",
    )(hidden, w_down, stream_in, w_qkv)
    return out[0], out[1]


def solution(mesh):
    placed = (P("row", "col"),) * 4
    return jax.shard_map(
        shards, mesh=mesh, in_specs=placed, out_specs=(P("row", "col"), P("row", "col")), check_vma=False
    )
```

```python
import jax
import jax.numpy as jnp
from jax import lax
from jax.experimental import pallas as pl
from jax.experimental.pallas import tpu as pltpu
from jax.sharding import PartitionSpec as P

MESH = pl.DeviceIdType.MESH
EPSILON = 1e-06
D_W = 4096
HEAD = 128
NX, NY, NZ = 4, 8, 8
F32 = jnp.float32
BF16 = jnp.bfloat16


def head_norm(parts):
    centre = parts - jnp.mean(parts, axis=-1, keepdims=True)
    spread = jnp.mean(centre * centre, axis=-1, keepdims=True)
    return centre * lax.rsqrt(spread + EPSILON)


def kernel(
    hid, wd, si, wq, out,
    wdg, ag, acc, p1, r1, sin, sg, st, stx, sty, wqg, p2, r2, ab, keep,
    s_hid, r_hid, s_si, r_si, s_a, r_a, s_wd, r_wd, s_wc, r_wc, s_wq, r_wq, s_qc, r_qc, own_sem,
    s_r1, r_r1, s_so, r_so, s_s, r_s, s_stx, r_stx, s_sty, r_sty, s_r2, r_r2, s_o, r_o,
):
    so, at = out.at[0], out.at[1]
    row, col = lax.axis_index("row"), lax.axis_index("col")
    z, x = lax.div(row, NX), lax.rem(row, NX)
    y, c = lax.div(col, 2), lax.rem(col, 2)
    xh, xl = lax.div(x, 2), lax.rem(x, 2)

    def dev(zz, xx, yy, cc):
        return (zz * NX + xx, yy * 2 + cc)

    def up(v, d, n):
        return lax.rem(v + d + n, n)

    sibling = dev(z, x, y, 1 - c)
    yn2 = (dev(z, x, up(y, 2, NY), c), dev(z, x, up(y, -2, NY), c))
    yn = (dev(z, x, up(y, 1, NY), c), dev(z, x, up(y, -1, NY), c))
    zn = (dev(up(z, 1, NZ), x, y, c), dev(up(z, -1, NZ), x, y, c))
    xgroup = [dev(z, up(x, d, NX), y, e) for d in range(NX) for e in (c, 1 - c)][1:]
    ygroup = [dev(z, x, up(y, d, NY), c) for d in range(1, NY)]
    away = (2, 1, 3)

    ends = []

    def remote(src, dst, ssem, rsem, to):
        copy = pltpu.make_async_remote_copy(
            src_ref=src, dst_ref=dst, send_sem=ssem, recv_sem=rsem, device_id=to, device_id_type=MESH
        )
        copy.start()
        ends.append((None, copy))

    def drain():
        for leaves, copy in ends:
            if leaves is None:
                copy.wait_send()
            else:

                @pl.when(leaves)
                def _(copy=copy):
                    copy.wait_send()

        ends.clear()

    def within(src, dst, ssem, rsem, tx, tc):
        leaves = (tx != x) | (tc != c)
        copy = pltpu.make_async_remote_copy(
            src_ref=src, dst_ref=dst, send_sem=ssem, recv_sem=rsem,
            device_id=dev(z, tx, y, tc), device_id_type=MESH,
        )

        @pl.when(leaves)
        def _():
            copy.start()

        @pl.when(jnp.logical_not(leaves))
        def _():
            pltpu.make_async_copy(src, dst, rsem).start()

        ends.append((leaves, copy))

    def arrived(dst, rsem):
        pltpu.make_async_remote_copy(
            src_ref=dst, dst_ref=dst, send_sem=rsem, recv_sem=rsem, device_id=sibling, device_id_type=MESH
        ).wait_recv()

    barrier = pltpu.get_barrier_semaphore()
    greet = xgroup + ygroup + list(zn)
    for d in greet:
        pl.semaphore_signal(barrier, inc=1, device_id=d, device_id_type=MESH)
    own = [pltpu.make_async_copy(wd, wdg.at[c, pl.ds(pl.multiple_of(z * 384, 128), 384)], own_sem.at[0])]
    for h in range(2):
        own.append(
            pltpu.make_async_copy(
                wq.at[:, pl.ds(h * 384, 384)],
                wqg.at[2 * c + h, pl.ds(pl.multiple_of(z * 128, 128), 128)],
                own_sem.at[1 + h],
            )
        )
    for copy in own:
        copy.start()
    own[0].wait()
    pl.semaphore_wait(barrier, len(greet))

    near = jnp.where(xh == c, xl, 1 - xl)
    half = (near, 1 - near)

    def wd_piece(j, p, k=c):
        return wdg.at[k, pl.ds(pl.multiple_of(j * 384 + p * 192, 64), 192)]

    def wq_piece(j, p, k=c):
        return wqg.at[2 * k + p, pl.ds(pl.multiple_of(j * 128, 128), 128)]

    def a_piece(j, p):
        return ag.at[j, pl.ds(pl.multiple_of(half[p // 2] * 128 + p % 2 * 64, 64), 64)]

    def s_piece(j, p):
        return sg.at[j, pl.ds(128 * p, 128)]

    def block(me, s, d):
        return up(me, -s if d == 0 else s, 8)

    def hop_send(piece, me, ssem, rsem, to, s, d, p, parts=2):
        j, k = block(me, s - 1, d), ((s - 1) * 2 + d) * parts + p
        remote(piece(j, p), piece(j, p), ssem.at[k], rsem.at[k], to[d])

    def hop(piece, me, ssem, rsem, to, s, p, parts=2):
        way = p * 2 // parts
        for d in (0, 1) if s < 4 else (way,):
            arrived(piece(block(me, s, d), p), rsem.at[((s - 1) * 2 + d) * parts + p])
            if s < 3 or (s == 3 and d == way):
                hop_send(piece, me, ssem, rsem, to, s + 1, d, p, parts)

    def share(piece, ssem, rsem, s, p):
        for d in (0, 1) if 0 < s < 4 else (p,):
            j, k = block(z, s, d), s * 4 + d * 2 + p
            remote(piece(j, p), piece(j, p), ssem.at[k], rsem.at[k], sibling)

    def shared(piece, rsem, s, p):
        for d in (0, 1) if 0 < s < 4 else (p,):
            arrived(piece(block(z, s, d), p, 1 - c), rsem.at[s * 4 + d * 2 + p])

    def wd_hop(s, p):
        hop(wd_piece, z, s_wd, r_wd, zn, s, p)
        share(wd_piece, s_wc, r_wc, s, p)

    def wq_start(d, p):
        hop_send(wq_piece, z, s_wq, r_wq, zn, 1, d, p)

    def wq_hop(s, ps=(0, 1)):
        for p in ps:
            hop(wq_piece, z, s_wq, r_wq, zn, s, p)
            share(wq_piece, s_qc, r_qc, s, p)

    def a_hop(s, p):
        for q in range(2):
            hop(a_piece, y, s_a, r_a, yn, s, 2 * p + q, 4)

    def a_start(p):
        for q in range(2):
            arrived(a_piece(y, 2 * p + q), r_hid.at[2 * half[p] + q])
            for d in range(2):
                hop_send(a_piece, y, s_a, r_a, yn, 1, d, 2 * p + q, 4)

    for p in range(2):
        for d in range(2):
            hop_send(wd_piece, z, s_wd, r_wd, zn, 1, d, p)
    for h in range(2):
        for q in range(2):
            within(
                hid.at[pl.ds(64 * q, 64), pl.ds(h * 384, 384)],
                ag.at[y, pl.ds(pl.multiple_of(xl * 128 + 64 * q, 64), 64)],
                s_hid.at[2 * h + q], r_hid.at[2 * xl + q], 2 * c + h, xh,
            )
    a_start(0)
    own[1].wait()
    own[2].wait()
    for p in range(2):
        share(wd_piece, s_wc, r_wc, 0, p)
    for h in range(2):
        within(si.at[:, pl.ds(h * 128, 128)], sin.at[xl], s_si.at[h], r_si.at[xl], 2 * c + h, xh)
    for s in range(1, 4):
        wd_hop(s, 0)
        if s > 1:
            a_hop(s - 1, 1)
        else:
            a_start(1)
        wd_hop(s, 1)
        if s > 1:
            for d in range(2):
                wq_start(d, s - 2)
        a_hop(s, 0)
    a_hop(3, 1)
    wq_hop(1, (0,))
    for s in range(4):
        for p in range(2):
            shared(wd_piece, r_wc, s, p)

    last_a, last_w = up(y, 4, 8), up(z, 4, 8)
    last_w = jnp.where(last_w == last_a, up(last_a, 1, 8), last_w)
    gap = up(last_w - last_a, 8, 8)

    def product(n, js, rows=slice(None)):
        a = jnp.concatenate([ag[j, rows] for j in js], axis=1)
        w = jnp.concatenate([wdg[n, pl.ds(pl.multiple_of(j * 384, 128), 384), :] for j in js], axis=0)
        return jnp.dot(a, w, preferred_element_type=F32)

    early = [up(last_a, k + (gap <= k).astype(jnp.int32), 8) for k in range(1, 7)]
    for n in range(2):
        acc[n] = product(n, early)
    for p in range(2):
        wd_hop(4, p)
    wq_hop(1, (1,))
    for p in range(2):
        shared(wd_piece, r_wc, 4, p)
    for p in range(2):
        a_hop(4, p)

    def features(tx):
        return pl.ds(pl.multiple_of(128 * tx, 128), 128)

    halves = (pl.ds(0, 128), pl.ds(128, 128))
    for t, rows in enumerate(halves):
        for n in range(2):
            late = product(n, [last_a, last_w], rows)
            p1[rows, pl.ds(256 * n, 256)] = (acc[n, rows] + late).astype(BF16)
        for k, d in enumerate(away):
            tx = up(x, d, NX)
            remote(
                p1.at[rows, features(tx)], r1.at[k, rows], s_r1.at[3 * t + k], r_r1.at[3 * t + k], dev(z, tx, y, c)
            )
    for p in range(2):
        share(wq_piece, s_qc, r_qc, 0, p)
    wq_hop(2)

    lanes = lax.broadcasted_iota(jnp.int32, (8, 128), 0)
    ones = jnp.ones((8, 128), BF16)

    def by_rows(v):
        return lax.dot_general(ones, v, (((1,), (1,)), ((), ())), preferred_element_type=F32)


    def s_send(j, s, d, p, to):
        k = (s - 1) * 4 + d * 2 + p
        remote(s_piece(j, p), s_piece(j, p), s_s.at[k], r_s.at[k], to[d])

    def s_hop(s, p):
        for d in (0, 1) if s < 4 else (p,):
            j = block(y, s, d)
            arrived(s_piece(j, p), r_s.at[(s - 1) * 4 + d * 2 + p])
            if s == 2:
                s_send(j, 3, d, p, yn)
                if d == p:
                    s_send(j, 4, d, p, yn2)

    tile = jnp.zeros((8, 128), F32)
    for t, rows in enumerate(halves):
        arrived(sin.at[t], r_si.at[t])
        for k in range(3):
            arrived(r1.at[k, rows], r_r1.at[3 * t + k])
        total = sin[t].astype(F32) + p1[rows, features(x)].astype(F32)
        for k in range(3):
            total += r1[k, rows, :].astype(F32)
        stream = total.astype(BF16)
        sg[y, rows, :] = stream
        for d in range(2):
            s_send(y, 2, d, t, yn2)
        for d in range(2):
            s_send(y, 1, d, t, yn)
        wide = stream.astype(F32)
        square = wide * wide
        high = square.astype(BF16)
        low = (square - high.astype(F32)).astype(BF16)
        sums, squares = by_rows(stream), by_rows(high) + by_rows(low)
        tile = jnp.where(lanes == t, sums, jnp.where(lanes == 2 + t, squares, tile))
    stx[3] = tile
    for k, d in enumerate(away):
        remote(stx.at[3], stx.at[k], s_stx.at[k], r_stx.at[k], dev(z, up(x, d, NX), y, c))
    wq_hop(3)
    s_hop(2, 0)
    for k in range(3):
        arrived(stx.at[k], r_stx.at[k])
    sty[y] = (stx[0] + stx[1]) + (stx[2] + stx[3])
    for n, d in enumerate(ygroup):
        remote(sty.at[y], sty.at[y], s_sty.at[n], r_sty.at[y], d)
    s_hop(2, 1)
    for t in range(2):
        within(s_piece(y, t), so.at[:, pl.ds(pl.multiple_of(128 * xl, 128), 128)], s_so.at[t], r_so.at[xl], 2 * c + t, xh)
    wq_hop(4)
    for s in (1, 3, 4):
        s_hop(s, 0)
    for n in range(1, NY):
        k = up(y, n, NY)
        arrived(sty.at[k], r_sty.at[k])
    stats = sty[0]
    for j in range(1, NY):
        stats += sty[j]
    means = stats[0:2] / D_W
    spreads = lax.rsqrt(stats[2:4] / D_W - means * means + EPSILON)
    st[...] = jnp.concatenate([means, spreads, jnp.zeros((124, 128), F32)], axis=0).T
    for s in range(5):
        for p in range(2):
            shared(wq_piece, r_qc, s, p)

    for t, rows in enumerate(halves):
        if t == 1:
            for s in (1, 3, 4):
                s_hop(s, 1)
        mean, rstd = st[:, t : t + 1], st[:, 2 + t : 3 + t]
        normed = jnp.concatenate(
            [((sg[j, rows, :].astype(F32) - mean) * rstd).astype(BF16) for j in range(NY)], axis=1
        )
        for k, d in enumerate(away):
            tx = up(x, d, NX)
            p2[k, rows, :] = jnp.dot(normed, wqg[tx], preferred_element_type=F32).astype(BF16)
            remote(p2.at[k, rows], r2.at[k, rows], s_r2.at[3 * t + k], r_r2.at[3 * t + k], dev(z, tx, y, c))
        keep[rows, :] = jnp.dot(normed, wqg[x], preferred_element_type=F32)
    sent = ends[-6:]
    del ends[-6:]
    drain()
    ends.extend(sent)
    queries, keys, values = [], [], []
    for t, rows in enumerate(halves):
        for k in range(3):
            arrived(r2.at[k, rows], r_r2.at[3 * t + k])
        total = keep[rows, :] + (r2[0, rows].astype(F32) + r2[1, rows].astype(F32)) + r2[2, rows].astype(F32)
        queries.append((head_norm(total[:, 0:128]) * (1.0 / HEAD**0.5)).astype(BF16))
        keys.append(head_norm(total[:, 128:256]).astype(BF16))
        values.append(total[:, 256:384].astype(BF16))
    keys, values = jnp.concatenate(keys, axis=0), jnp.concatenate(values, axis=0)
    for t, rows in enumerate(halves):
        scores = lax.dot_general(queries[t], keys, (((1,), (1,)), ((), ())), preferred_element_type=F32)
        expon = jnp.exp(scores)
        probs = (expon / jnp.sum(expon, axis=-1, keepdims=True)).astype(BF16)
        ab[rows, :] = jnp.dot(probs, values, preferred_element_type=F32).astype(BF16)
        within(
            ab.at[rows], at.at[:, pl.ds(pl.multiple_of(128 * xl, 128), 128)],
            s_o.at[t], r_o.at[xl], 2 * c + t, xh,
        )

    for h in range(2):
        arrived(so.at[:, pl.ds(128 * h, 128)], r_so.at[h])
        arrived(at.at[:, pl.ds(128 * h, 128)], r_o.at[h])
    drain()


def shards(hidden, w_down, stream_in, w_qkv):
    vm = lambda *n: pltpu.VMEM(n, BF16)
    fm = lambda *n: pltpu.VMEM(n, F32)
    counts = (4, 4, 2, 2, 32, 32, 16, 16, 20, 20, 16, 16, 20, 20, 3, 6, 6, 2, 2, 16, 16, 3, 3, 7, 8, 6, 6, 2, 2)
    out = pl.pallas_call(
        kernel,
        out_shape=pltpu.VMEM((2, 128, 256), BF16),
        in_specs=[pl.BlockSpec(memory_space=pltpu.HBM)] * 4,
        out_specs=pl.BlockSpec(memory_space=pltpu.VMEM),
        scratch_shapes=[
            vm(2, 3072, 256), vm(8, 256, 384), fm(2, 256, 256), vm(256, 512), vm(3, 256, 128), vm(2, 128, 128),
            vm(8, 256, 128), fm(128, 128), fm(4, 8, 128), fm(8, 8, 128), vm(4, 1024, 384), vm(3, 256, 384),
            vm(3, 256, 384), vm(256, 128), fm(256, 384),
            *(pltpu.SemaphoreType.DMA((n,)) for n in counts),
        ],
        compiler_params=pltpu.CompilerParams(
            collective_id=0, has_side_effects=True, vmem_limit_bytes=56 * 1024 * 1024
        ),
        cost_estimate=pl.CostEstimate(flops=1_700_000_000, bytes_accessed=1_000_000, transcendentals=65536),
        name="layer",
    )(hidden, w_down, stream_in, w_qkv)
    return out[0], out[1]


def solution(mesh):
    placed = (P("row", "col"),) * 4
    return jax.shard_map(
        shards, mesh=mesh, in_specs=placed, out_specs=(P("row", "col"), P("row", "col")), check_vma=False
    )
```

```python
import jax
import jax.numpy as jnp
from jax import lax
from jax.experimental import pallas as pl
from jax.experimental.pallas import tpu as pltpu
from jax.sharding import PartitionSpec as P

MESH = pl.DeviceIdType.MESH
EPSILON = 1e-06
D_W = 4096
HEAD = 128
NX, NY, NZ = 4, 8, 8
F32 = jnp.float32
BF16 = jnp.bfloat16


def head_norm(parts):
    centre = parts - jnp.mean(parts, axis=-1, keepdims=True)
    spread = jnp.mean(centre * centre, axis=-1, keepdims=True)
    return centre * lax.rsqrt(spread + EPSILON)


def kernel(
    hid, wd, si, wq, out,
    wdg, ag, acc, p1, r1, sin, sg, st, stx, sty, wqg, p2, r2, ab, keep,
    s_hid, r_hid, s_si, r_si, s_a, r_a, s_wd, r_wd, s_wc, r_wc, s_wq, r_wq, s_qc, r_qc, own_sem,
    s_r1, r_r1, s_so, r_so, s_s, r_s, s_stx, r_stx, s_sty, r_sty, s_r2, r_r2, s_o, r_o,
):
    so, at = out.at[0], out.at[1]
    row, col = lax.axis_index("row"), lax.axis_index("col")
    z, x = lax.div(row, NX), lax.rem(row, NX)
    y, c = lax.div(col, 2), lax.rem(col, 2)
    xh, xl = lax.div(x, 2), lax.rem(x, 2)

    def dev(zz, xx, yy, cc):
        return (zz * NX + xx, yy * 2 + cc)

    def up(v, d, n):
        return lax.rem(v + d + n, n)

    sibling = dev(z, x, y, 1 - c)
    yn2 = (dev(z, x, up(y, 2, NY), c), dev(z, x, up(y, -2, NY), c))
    yn = (dev(z, x, up(y, 1, NY), c), dev(z, x, up(y, -1, NY), c))
    zn = (dev(up(z, 1, NZ), x, y, c), dev(up(z, -1, NZ), x, y, c))
    xgroup = [dev(z, up(x, d, NX), y, e) for d in range(NX) for e in (c, 1 - c)][1:]
    ygroup = [dev(z, x, up(y, d, NY), c) for d in range(1, NY)]
    away = (2, 1, 3)

    ends = []

    def remote(src, dst, ssem, rsem, to):
        copy = pltpu.make_async_remote_copy(
            src_ref=src, dst_ref=dst, send_sem=ssem, recv_sem=rsem, device_id=to, device_id_type=MESH
        )
        copy.start()
        ends.append((None, copy))

    def drain():
        for leaves, copy in ends:
            if leaves is None:
                copy.wait_send()
            else:

                @pl.when(leaves)
                def _(copy=copy):
                    copy.wait_send()

        ends.clear()

    def within(src, dst, ssem, rsem, tx, tc):
        leaves = (tx != x) | (tc != c)
        copy = pltpu.make_async_remote_copy(
            src_ref=src, dst_ref=dst, send_sem=ssem, recv_sem=rsem,
            device_id=dev(z, tx, y, tc), device_id_type=MESH,
        )

        @pl.when(leaves)
        def _():
            copy.start()

        @pl.when(jnp.logical_not(leaves))
        def _():
            pltpu.make_async_copy(src, dst, rsem).start()

        ends.append((leaves, copy))

    def arrived(dst, rsem):
        pltpu.make_async_remote_copy(
            src_ref=dst, dst_ref=dst, send_sem=rsem, recv_sem=rsem, device_id=sibling, device_id_type=MESH
        ).wait_recv()

    barrier = pltpu.get_barrier_semaphore()
    greet = xgroup + ygroup + list(zn)
    for d in greet:
        pl.semaphore_signal(barrier, inc=1, device_id=d, device_id_type=MESH)
    own = [pltpu.make_async_copy(wd, wdg.at[c, pl.ds(pl.multiple_of(z * 384, 128), 384)], own_sem.at[0])]
    for h in range(2):
        own.append(
            pltpu.make_async_copy(
                wq.at[:, pl.ds(h * 384, 384)],
                wqg.at[2 * c + h, pl.ds(pl.multiple_of(z * 128, 128), 128)],
                own_sem.at[1 + h],
            )
        )
    for copy in own:
        copy.start()
    own[0].wait()
    pl.semaphore_wait(barrier, len(greet))

    near = jnp.where(xh == c, xl, 1 - xl)
    half = (near, 1 - near)

    def wd_piece(j, p, k=c):
        return wdg.at[k, pl.ds(pl.multiple_of(j * 384 + p * 192, 64), 192)]

    def wd_block(j, k=c):
        return wdg.at[k, pl.ds(pl.multiple_of(j * 384, 128), 384)]

    def wq_piece(j, p, k=c):
        return wqg.at[2 * k + p, pl.ds(pl.multiple_of(j * 128, 128), 128)]

    def a_piece(j, p):
        return ag.at[j, pl.ds(pl.multiple_of(half[p // 2] * 128 + p % 2 * 64, 64), 64)]

    def s_piece(j, p):
        return sg.at[j, pl.ds(128 * p, 128)]

    def block(me, s, d):
        return up(me, -s if d == 0 else s, 8)

    def hop_send(piece, me, ssem, rsem, to, s, d, p, parts=2):
        j, k = block(me, s - 1, d), ((s - 1) * 2 + d) * parts + p
        remote(piece(j, p), piece(j, p), ssem.at[k], rsem.at[k], to[d])

    def hop(piece, me, ssem, rsem, to, s, p, parts=2):
        way = p * 2 // parts
        for d in (0, 1) if s < 4 else (way,):
            arrived(piece(block(me, s, d), p), rsem.at[((s - 1) * 2 + d) * parts + p])
            if s < 3 or (s == 3 and d == way):
                hop_send(piece, me, ssem, rsem, to, s + 1, d, p, parts)

    def share(piece, ssem, rsem, s, p):
        for d in (0, 1) if 0 < s < 4 else (p,):
            j, k = block(z, s, d), s * 4 + d * 2 + p
            remote(piece(j, p), piece(j, p), ssem.at[k], rsem.at[k], sibling)

    def shared(piece, rsem, s, p):
        for d in (0, 1) if 0 < s < 4 else (p,):
            arrived(piece(block(z, s, d), p, 1 - c), rsem.at[s * 4 + d * 2 + p])

    def wd_hop(s, p):
        hop(wd_piece, z, s_wd, r_wd, zn, s, p)
        if s == 4:
            share(wd_piece, s_wc, r_wc, s, p)
        elif p == 1:
            for d in range(2):
                j, k = block(z, s, d), s * 4 + d * 2
                remote(wd_block(j), wd_block(j), s_wc.at[k], r_wc.at[k], sibling)

    def wq_start(d, p):
        hop_send(wq_piece, z, s_wq, r_wq, zn, 1, d, p)

    def wq_hop(s, ps=(0, 1)):
        for p in ps:
            hop(wq_piece, z, s_wq, r_wq, zn, s, p)
            share(wq_piece, s_qc, r_qc, s, p)

    def a_hop(s, p):
        for q in range(2):
            hop(a_piece, y, s_a, r_a, yn, s, 2 * p + q, 4)

    def a_start(p):
        for q in range(2):
            arrived(a_piece(y, 2 * p + q), r_hid.at[2 * half[p] + q])
            for d in range(2):
                hop_send(a_piece, y, s_a, r_a, yn, 1, d, 2 * p + q, 4)

    for h in range(2):
        for q in range(2):
            within(
                hid.at[pl.ds(64 * q, 64), pl.ds(h * 384, 384)],
                ag.at[y, pl.ds(pl.multiple_of(xl * 128 + 64 * q, 64), 64)],
                s_hid.at[2 * h + q], r_hid.at[2 * xl + q], 2 * c + h, xh,
            )
    for p in range(2):
        for d in range(2):
            hop_send(wd_piece, z, s_wd, r_wd, zn, 1, d, p)
    a_start(0)
    a_start(1)
    own[1].wait()
    own[2].wait()
    for p in range(2):
        share(wd_piece, s_wc, r_wc, 0, p)
    for h in range(2):
        within(si.at[:, pl.ds(h * 128, 128)], sin.at[xl], s_si.at[h], r_si.at[xl], 2 * c + h, xh)
    for s in range(1, 4):
        wd_hop(s, 0)
        if s > 1:
            a_hop(s - 1, 1)
        wd_hop(s, 1)
        if s > 1:
            for d in range(2):
                wq_start(d, s - 2)
        a_hop(s, 0)
    a_hop(3, 1)
    wq_hop(1, (0,))
    for p in range(2):
        shared(wd_piece, r_wc, 0, p)
    for s in range(1, 4):
        for d in range(2):
            arrived(wd_block(block(z, s, d), 1 - c), r_wc.at[s * 4 + d * 2])

    last_a, last_w = up(y, 4, 8), up(z, 4, 8)
    last_w = jnp.where(last_w == last_a, up(last_a, 1, 8), last_w)
    gap = up(last_w - last_a, 8, 8)

    def product(n, js, rows=slice(None)):
        a = jnp.concatenate([ag[j, rows] for j in js], axis=1)
        w = jnp.concatenate([wdg[n, pl.ds(pl.multiple_of(j * 384, 128), 384), :] for j in js], axis=0)
        return jnp.dot(a, w, preferred_element_type=F32)

    early = [up(last_a, k + (gap <= k).astype(jnp.int32), 8) for k in range(1, 7)]
    for n in range(2):
        acc[n] = product(n, early)
    for p in range(2):
        wd_hop(4, p)
    wq_hop(1, (1,))
    for p in range(2):
        shared(wd_piece, r_wc, 4, p)
    for p in range(2):
        a_hop(4, p)

    def features(tx):
        return pl.ds(pl.multiple_of(128 * tx, 128), 128)

    halves = (pl.ds(0, 128), pl.ds(128, 128))
    for t, rows in enumerate(halves):
        for n in range(2):
            late = product(n, [last_a, last_w], rows)
            p1[rows, pl.ds(256 * n, 256)] = (acc[n, rows] + late).astype(BF16)
        for k, d in enumerate(away):
            tx = up(x, d, NX)
            remote(
                p1.at[rows, features(tx)], r1.at[k, rows], s_r1.at[3 * t + k], r_r1.at[3 * t + k], dev(z, tx, y, c)
            )
    for p in range(2):
        share(wq_piece, s_qc, r_qc, 0, p)
    wq_hop(2)

    lanes = lax.broadcasted_iota(jnp.int32, (8, 128), 0)
    ones = jnp.ones((8, 128), BF16)

    def by_rows(v):
        return lax.dot_general(ones, v, (((1,), (1,)), ((), ())), preferred_element_type=F32)


    def s_send(j, s, d, p, to):
        k = (s - 1) * 4 + d * 2 + p
        remote(s_piece(j, p), s_piece(j, p), s_s.at[k], r_s.at[k], to[d])

    def s_hop(s, p):
        for d in (0, 1) if s < 4 else (p,):
            j = block(y, s, d)
            arrived(s_piece(j, p), r_s.at[(s - 1) * 4 + d * 2 + p])
            if s == 2:
                s_send(j, 3, d, p, yn)
                if d == p:
                    s_send(j, 4, d, p, yn2)

    tile = jnp.zeros((8, 128), F32)
    for t, rows in enumerate(halves):
        arrived(sin.at[t], r_si.at[t])
        for k in range(3):
            arrived(r1.at[k, rows], r_r1.at[3 * t + k])
        total = sin[t].astype(F32) + p1[rows, features(x)].astype(F32)
        for k in range(3):
            total += r1[k, rows, :].astype(F32)
        stream = total.astype(BF16)
        sg[y, rows, :] = stream
        for d in range(2):
            s_send(y, 2, d, t, yn2)
        for d in range(2):
            s_send(y, 1, d, t, yn)
        wide = stream.astype(F32)
        square = wide * wide
        high = square.astype(BF16)
        low = (square - high.astype(F32)).astype(BF16)
        sums, squares = by_rows(stream), by_rows(high) + by_rows(low)
        tile = jnp.where(lanes == t, sums, jnp.where(lanes == 2 + t, squares, tile))
    stx[3] = tile
    for k, d in enumerate(away):
        remote(stx.at[3], stx.at[k], s_stx.at[k], r_stx.at[k], dev(z, up(x, d, NX), y, c))
    wq_hop(3)
    s_hop(2, 0)
    for k in range(3):
        arrived(stx.at[k], r_stx.at[k])
    sty[y] = (stx[0] + stx[1]) + (stx[2] + stx[3])
    for n, d in enumerate(ygroup):
        remote(sty.at[y], sty.at[y], s_sty.at[n], r_sty.at[y], d)
    s_hop(2, 1)
    for t in range(2):
        within(s_piece(y, t), so.at[:, pl.ds(pl.multiple_of(128 * xl, 128), 128)], s_so.at[t], r_so.at[xl], 2 * c + t, xh)
    wq_hop(4)
    for s in (1, 3, 4):
        s_hop(s, 0)
    for n in range(1, NY):
        k = up(y, n, NY)
        arrived(sty.at[k], r_sty.at[k])
    stats = sty[0]
    for j in range(1, NY):
        stats += sty[j]
    means = stats[0:2] / D_W
    spreads = lax.rsqrt(stats[2:4] / D_W - means * means + EPSILON)
    st[...] = jnp.concatenate([means, spreads, jnp.zeros((124, 128), F32)], axis=0).T
    for s in range(5):
        for p in range(2):
            shared(wq_piece, r_qc, s, p)

    for t, rows in enumerate(halves):
        if t == 1:
            for s in (1, 3, 4):
                s_hop(s, 1)
        mean, rstd = st[:, t : t + 1], st[:, 2 + t : 3 + t]
        normed = jnp.concatenate(
            [((sg[j, rows, :].astype(F32) - mean) * rstd).astype(BF16) for j in range(NY)], axis=1
        )
        for k, d in enumerate(away):
            tx = up(x, d, NX)
            p2[k, rows, :] = jnp.dot(normed, wqg[tx], preferred_element_type=F32).astype(BF16)
            remote(p2.at[k, rows], r2.at[k, rows], s_r2.at[3 * t + k], r_r2.at[3 * t + k], dev(z, tx, y, c))
        keep[rows, :] = jnp.dot(normed, wqg[x], preferred_element_type=F32)
    sent = ends[-6:]
    del ends[-6:]
    drain()
    ends.extend(sent)
    for t, rows in enumerate(halves):
        for k in range(3):
            arrived(r2.at[k, rows], r_r2.at[3 * t + k])
        keep[rows, :] += (r2[0, rows].astype(F32) + r2[1, rows].astype(F32)) + r2[2, rows].astype(F32)
    total = keep[...]
    keys = head_norm(total[:, 128:256]).astype(BF16)
    values = total[:, 256:384].astype(BF16)
    for t in range(2):
        queries = (head_norm(total[128 * t : 128 * t + 128, 0:128]) * (1.0 / HEAD**0.5)).astype(BF16)
        scores = lax.dot_general(queries, keys, (((1,), (1,)), ((), ())), preferred_element_type=F32)
        expon = jnp.exp(scores)
        probs = (expon / jnp.sum(expon, axis=-1, keepdims=True)).astype(BF16)
        ab[pl.ds(128 * t, 128), :] = jnp.dot(probs, values, preferred_element_type=F32).astype(BF16)
        within(
            ab.at[pl.ds(128 * t, 128)], at.at[:, pl.ds(pl.multiple_of(128 * xl, 128), 128)],
            s_o.at[t], r_o.at[xl], 2 * c + t, xh,
        )

    for h in range(2):
        arrived(so.at[:, pl.ds(128 * h, 128)], r_so.at[h])
        arrived(at.at[:, pl.ds(128 * h, 128)], r_o.at[h])
    drain()


def shards(hidden, w_down, stream_in, w_qkv):
    vm = lambda *n: pltpu.VMEM(n, BF16)
    fm = lambda *n: pltpu.VMEM(n, F32)
    counts = (4, 4, 2, 2, 32, 32, 16, 16, 20, 20, 16, 16, 20, 20, 3, 6, 6, 2, 2, 16, 16, 3, 3, 7, 8, 6, 6, 2, 2)
    out = pl.pallas_call(
        kernel,
        out_shape=pltpu.VMEM((2, 128, 256), BF16),
        in_specs=[pl.BlockSpec(memory_space=pltpu.HBM)] * 4,
        out_specs=pl.BlockSpec(memory_space=pltpu.VMEM),
        scratch_shapes=[
            vm(2, 3072, 256), vm(8, 256, 384), fm(2, 256, 256), vm(256, 512), vm(3, 256, 128), vm(2, 128, 128),
            vm(8, 256, 128), fm(128, 128), fm(4, 8, 128), fm(8, 8, 128), vm(4, 1024, 384), vm(3, 256, 384),
            vm(3, 256, 384), vm(256, 128), fm(256, 384),
            *(pltpu.SemaphoreType.DMA((n,)) for n in counts),
        ],
        compiler_params=pltpu.CompilerParams(
            collective_id=0, has_side_effects=True, vmem_limit_bytes=56 * 1024 * 1024
        ),
        cost_estimate=pl.CostEstimate(flops=1_700_000_000, bytes_accessed=1_000_000, transcendentals=65536),
        name="layer",
    )(hidden, w_down, stream_in, w_qkv)
    return out[0], out[1]


def solution(mesh):
    placed = (P("row", "col"),) * 4
    return jax.shard_map(
        shards, mesh=mesh, in_specs=placed, out_specs=(P("row", "col"), P("row", "col")), check_vma=False
    )
```
